512 devices in a mesh: rep: 32 (over y, x, core), shard: 16 (over z).
Axes of the slice: x: 4, y: 4, z: 16, core: 2. Of those that a mesh axis runs over, the one named last changes fastest.
Arguments:
- activations: bfloat16 [32, 2048, 4096], P('rep', None, 'shard'), may hold values from -6 to 6
- output_grad: bfloat16 [32, 2048, 1664], P('rep', 'shard'), may hold values from -0.125 to 0.125
- feedback: bfloat16 [32, 4096, 1664], P('rep', 'shard'), may hold values from -4 to 4
- right_start: float32 [1664, 32], replicated, may hold values from -6 to 6
Outputs:
- averaged: bfloat16 [4096, 1664], P('shard')
- feedback_next: bfloat16 [32, 4096, 1664], P('rep', 'shard')
- right_factor: float32 [1664, 32], replicated
The draws below stay inside these ranges and needn't reach their ends.
All inputs are finite; a program needn't handle non-finite values.
Results may differ from the reference program's by a relative error of at most 0.0013.
Values may be sent and summed in bfloat16 or wider, within the bound.
A program may use at most 64 MiB of HBM per device.

```python
import jax
import jax.numpy as jnp
from jax import lax

D = 1664
HID = 4096
RANK = 32
TOK_GROUP = 2048
N_REP = 32


def steps_of(own_key, dims, cuts, smallest, top_value):
    def one(axis_at, blocks):
        heights = jax.random.uniform(jax.random.fold_in(jax.random.fold_in(own_key, 6), axis_at), (blocks,), jnp.float32, smallest / len(cuts), top_value / len(cuts))
        return jnp.repeat(jnp.exp(heights), dims[axis_at] // blocks).reshape((-1,) + (1,) * (len(dims) - axis_at - 1))

    level = one(*cuts[0])
    for cut in cuts[1:]:
        level = level * one(*cut)
    return level


def bell_draw(own_key, shape, spread, most, cuts=(), held_as=jnp.bfloat16):
    gain = steps_of(own_key, shape, cuts, -0.22, 0.18) if cuts else 1.0
    drawn = jax.random.normal(own_key, shape, jnp.float32) * spread * gain
    return jnp.minimum(jnp.maximum(drawn, -most), most).astype(held_as)


def setup_inputs(seed: int = 0) -> dict:
    key_list = jax.random.split(jax.random.key(seed), 5)
    return {
        "activations": bell_draw(key_list[0], (N_REP, TOK_GROUP, HID), 1.0, 6.0, ((0, 32), (2, 16))),
        "output_grad": bell_draw(key_list[1], (N_REP, TOK_GROUP, D), TOK_GROUP ** -0.5, 0.125, ((0, 32), (1, 16))),
        "feedback": bell_draw(key_list[2], (N_REP, HID, D), 0.5, 4.0, ((0, 32), (1, 16))),
        "right_start": bell_draw(key_list[3], (D, RANK), 1.0, 6.0, (), jnp.float32),
    }


def reference(activations, output_grad, feedback, right_start):
    highest = lax.Precision.HIGHEST

    def merged_of(replica):
        left = activations[replica].astype(jnp.float32)
        right = output_grad[replica].astype(jnp.float32)
        gradient = jnp.dot(left.T.astype(jnp.float32), right.astype(jnp.float32), precision=highest, preferred_element_type=jnp.float32)
        return gradient + feedback[replica].astype(jnp.float32)
    merged = lax.map(merged_of, jnp.arange(N_REP, dtype=jnp.int32))
    projected = jnp.einsum('rhd,dk->hk', merged, right_start, precision=highest)
    gram_matrix = jnp.dot(projected.T, projected, precision=highest)
    cholesky_factor = jnp.linalg.cholesky(gram_matrix)
    orthonormal = jax.scipy.linalg.solve_triangular(cholesky_factor, projected.T, lower=True).T
    right_factor = jnp.einsum('rhd,hk->dk', merged, orthonormal, precision=highest) / N_REP
    rebuilt = jnp.dot(orthonormal, right_factor.T, precision=highest)
    averaged = rebuilt.astype(jnp.bfloat16)
    feedback_next = (merged - rebuilt[None]).astype(jnp.bfloat16)
    return (averaged, feedback_next, right_factor)
```

```python
import jax
import jax.numpy as jnp
from jax import lax
from jax.experimental import pallas as pl
from jax.experimental.pallas import tpu as pltpu
from jax.sharding import PartitionSpec as P

MESH = pl.DeviceIdType.MESH
F32, BF16 = jnp.float32, jnp.bfloat16
NZ, NR = 16, 32
TB, D, H, K = 128, 1664, 256, 32
PARTS = 2
ROWS = TB // PARTS
HELD = 5
P_OWNERS = 8
W_OWNERS = 26
NN = (((1,), (0,)), ((), ()))
NT = (((1,), (1,)), ((), ()))
TN = (((0,), (0,)), ((), ()))


def mm(a, b, dims):
    return lax.dot_general(a, b, dims, preferred_element_type=F32)


def split3(x):
    hi = x.astype(BF16)
    rest = x - hi.astype(F32)
    mid = rest.astype(BF16)
    low = (rest - mid.astype(F32)).astype(BF16)
    return hi, mid, low


def stack3(x):
    return jnp.concatenate(split3(x), axis=0)


def fold3(x):
    n = x.shape[0] // 3
    return x[:n] + (x[n : 2 * n] + x[2 * n :])


def columns(body):
    def step(i, carry):
        body(pl.ds(pl.multiple_of(i * 256, 256), 256))
        return carry

    lax.fori_loop(0, 6, step, 0)
    body(pl.ds(1536, 128))


def inverse_factor(packed):
    lane = lax.broadcasted_iota(jnp.int32, (8, 128), 1)
    sub = lax.broadcasted_iota(jnp.int32, (8, 128), 0)
    rows = []
    for q in range(4):
        g = pltpu.roll(packed, (32 - 32 * q) % 128, 1) if q != 1 else packed
        g = jnp.where((lane >= 32) & (lane < 64), g, 0.0)
        rows.append(g + jnp.where(lane == sub + 8 * q, 1.0, 0.0))
    for k in range(K):
        q, i = k // 8, k % 8
        row = rows[q][i : i + 1, :]
        pivot = row[:, 32 + k : 33 + k]
        inv = lax.rsqrt(pivot)
        inv = inv * (1.5 - 0.5 * pivot * inv * inv)
        row = row * inv
        for t in range(q, 4):
            col = rows[t][:, 32 + k : 33 + k] * inv
            new = rows[t] - col * row
            if t == q:
                new = jnp.where(sub > i, new, jnp.where(sub == i, row, rows[t]))
            rows[t] = new
    return jnp.concatenate(rows, axis=0)[:, 0:K]


def kernel(
    a_ref, b_ref, f_ref, r_ref, avg_ref, next_ref, rf_ref,
    ball, av, fv, rv, acc, br, psend, prs, ptot, gsend, grecv, ot,
    usend, urecv, wsend, wrs, wz, zrs, wfin,
    lsem, ssem, rsem, br_s, br_r, u_s, u_r, one_s, one_r,
):
    z = lax.axis_index("shard")
    me = lax.axis_index("rep")

    def zat(off):
        return lax.rem(z + (off + 2 * NZ), NZ)

    def block(owner):
        return pl.ds(pl.multiple_of(owner * TB, TB), TB)

    loads = [
        pltpu.make_async_copy(b_ref.at[0], ball.at[block(z)], lsem.at[0]),
        pltpu.make_async_copy(r_ref, rv, lsem.at[1]),
        pltpu.make_async_copy(f_ref.at[0], fv, lsem.at[2]),
        pltpu.make_async_copy(a_ref.at[0], av, lsem.at[3]),
    ]
    for load in loads:
        load.start()

    barrier = pltpu.get_barrier_semaphore()

    @pl.loop(1, NZ)
    def _(d):
        pl.semaphore_signal(barrier, inc=1, device_id={"shard": lax.rem(z + d, NZ)}, device_id_type=MESH)

    @pl.loop(1, NR)
    def _(d):
        pl.semaphore_signal(barrier, inc=1, device_id={"rep": lax.rem(me + d, NR)}, device_id_type=MESH)

    def wait_bytes(ref, sem):
        pltpu.make_async_copy(ref, ref, sem).wait()

    def piece(owner, part):
        return ball.at[pl.ds(pl.multiple_of(owner * TB + part * ROWS, ROWS), ROWS)]

    def ring(way, s, part):
        owner, to = (zat(-s), zat(1)) if way == 0 else (zat(s), zat(-1))
        return pltpu.make_async_remote_copy(
            piece(owner, part), piece(owner, part), ssem.at[way, s, part], rsem.at[way, s, part],
            device_id={"shard": to}, device_id_type=MESH,
        )

    def used(way, s, part):
        return s < 7 or (s == 7 and (part == 0) == (way == 0))

    def tick(k):
        s = k // PARTS
        for way in range(2):
            part = k % PARTS if way == 0 else PARTS - 1 - k % PARTS
            if used(way, s, part):
                ring(way, s, part).wait_recv()
                if used(way, s + 1, part):
                    ring(way, s + 1, part).start()

    def gather_terms(offsets):
        at = jnp.concatenate([av[block(zat(o)), :].T for o in offsets], axis=1)

        def body(cols):
            rows = jnp.concatenate([ball[block(zat(o)), cols] for o in offsets], axis=0)
            acc[:, cols] += mm(at, rows, NN)

        columns(body)

    loads[0].wait()
    loads[1].wait()
    r3 = stack3(rv[...])
    br[:, block(z)] = fold3(mm(r3, ball[block(z), :], NT))
    pl.semaphore_wait(barrier, NZ - 1 + NR - 1)

    for k in range(PARTS):
        for way in range(2):
            ring(way, 0, k if way == 0 else PARTS - 1 - k).start()

    def br_copy(d):
        return pltpu.make_async_remote_copy(
            br.at[:, block(z)], br.at[:, block(z)], br_s, br_r,
            device_id={"shard": lax.rem(z + d, NZ)}, device_id_type=MESH,
        )

    @pl.loop(1, NZ)
    def _(d):
        br_copy(d).start()

    loads[2].wait()
    fr = fold3(mm(r3, fv[...], NT))
    columns(lambda cols: acc.__setitem__((slice(None), cols), fv[:, cols].astype(F32)))
    loads[3].wait()
    wait_bytes(br.at[:, pl.ds(0, (NZ - 1) * TB)], br_r)
    psend[...] = fr + fold3(mm(stack3(br[...]), av[...], NN))

    def p_tile(o):
        return (
            pl.ds(pl.multiple_of(o // 2 * 8, 8), 8),
            pl.ds(pl.multiple_of(o % 2 * 128, 128), 128),
        )

    @pl.loop(0, P_OWNERS)
    def _(o):
        to = 4 * o

        @pl.when(to != me)
        def _():
            pltpu.make_async_remote_copy(
                psend.at[p_tile(o)], prs.at[lax.rem(me - to + (NR - 1), NR)], one_s.at[0], one_r.at[0],
                device_id={"rep": to}, device_id_type=MESH,
            ).start()

    tick(0)
    gather_terms([0])
    own_p = lax.rem(me, 4) == 0

    @pl.when(own_p)
    def _():
        wait_bytes(prs.at[pl.ds(0, NR - 1)], one_r.at[0])
        tile = p_tile(me // 4)
        ptot[tile] = jnp.sum(prs[0 : NR - 1], axis=0) + psend[tile]

        @pl.loop(1, NR)
        def _(d):
            pltpu.make_async_remote_copy(
                ptot.at[tile], ptot.at[tile], one_s.at[1], one_r.at[1],
                device_id={"rep": lax.rem(me + d, NR)}, device_id_type=MESH,
            ).start()

    tick(1)
    gather_terms([-1, 1])

    @pl.when(own_p)
    def _():
        wait_bytes(prs.at[pl.ds(0, P_OWNERS - 1)], one_r.at[1])

    @pl.when(jnp.logical_not(own_p))
    def _():
        wait_bytes(prs.at[pl.ds(0, P_OWNERS)], one_r.at[1])

    pt = ptot[...]
    p_hi, p_mid, p_low = split3(pt)
    wide = jnp.concatenate([pt] * 4, axis=0)
    w_hi, w_mid, w_low = split3(wide)
    g = mm(p_hi, w_hi, NT) + (
        (mm(p_hi, w_mid, NT) + mm(p_mid, w_hi, NT))
        + (mm(p_mid, w_mid, NT) + mm(p_hi, w_low, NT) + mm(p_low, w_hi, NT))
    )
    lane = lax.broadcasted_iota(jnp.int32, (8, 128), 1)
    packed = jnp.zeros((8, 128), F32)
    for q in range(4):
        packed = jnp.where((lane >= 32 * q) & (lane < 32 * q + 32), g[8 * q : 8 * q + 8], packed)
    gsend[...] = packed

    @pl.loop(1, NZ)
    def _(d):
        pltpu.make_async_remote_copy(
            gsend, grecv.at[d - 1], one_s.at[2], one_r.at[2],
            device_id={"shard": lax.rem(z + d, NZ)}, device_id_type=MESH,
        ).start()

    tick(2)
    wait_bytes(grecv.at[pl.ds(0, NZ - 1)], one_r.at[2])
    l_inv = inverse_factor(jnp.sum(grecv[0 : NZ - 1], axis=0) + gsend[...])
    tick(3)
    l_hi, l_mid, l_low = split3(l_inv)
    o_t = mm(l_hi, p_hi, NN) + (
        (mm(l_hi, p_mid, NN) + mm(l_mid, p_hi, NN))
        + (mm(l_mid, p_mid, NN) + mm(l_hi, p_low, NN) + mm(l_low, p_hi, NN))
    )
    ot[...] = o_t
    o3 = stack3(o_t)

    hops = [(o, o - HELD) for o in range(HELD + 1, 9)] + [(-o, HELD - o) for o in range(HELD + 1, 8)]

    def u_copy(i):
        return pltpu.make_async_remote_copy(
            usend.at[i], urecv.at[i], u_s.at[i], u_r.at[i],
            device_id={"shard": zat(hops[i][1])}, device_id_type=MESH,
        )

    for i, (o, _) in enumerate(hops):
        usend[i] = fold3(mm(o3, av[block(zat(o)), :], NT))
        u_copy(i).start()
    gather_terms([-2, 2])
    for s in range(3, HELD + 1):
        tick(2 * s - 2)
        tick(2 * s - 1)
        gather_terms([-s, s])
    for i in range(len(hops)):
        u_copy(i).wait_recv()
    u_up = sum(urecv[i] for i in range(len(hops)) if hops[i][0] > 0)
    u_down = sum(urecv[i] for i in range(len(hops)) if hops[i][0] < 0)
    u3 = stack3(jnp.concatenate([u_up, u_down], axis=1))

    def w_terms(cols):
        m_hi, m_mid, _ = split3(acc[:, cols])
        rows = jnp.concatenate([ball[block(zat(HELD)), cols], ball[block(zat(-HELD)), cols]], axis=0)
        total = mm(o3, m_hi, NN) + mm(u3, rows, NN)
        cross = mm(o3[: 2 * K], m_mid, NN)
        wsend[:, cols] = fold3(total) + (cross[:K] + cross[K:])

    columns(w_terms)

    def w_chunk(q):
        return (
            pl.ds(pl.multiple_of(lax.rem(q, 2) * 16, 16), 16),
            pl.ds(pl.multiple_of(q // 2 * 128, 128), 128),
        )

    @pl.loop(0, W_OWNERS)
    def _(q):
        @pl.when(q != me)
        def _():
            pltpu.make_async_remote_copy(
                wsend.at[w_chunk(q)], wrs.at[lax.rem(me - q + (NR - 1), NR)], one_s.at[3], one_r.at[3],
                device_id={"rep": q}, device_id_type=MESH,
            ).start()

    tick(2 * HELD)
    own_w = me < W_OWNERS
    base = lax.rem(me, 8)
    which = z // 8
    own_z = own_w & (lax.rem(z, 8) == base)
    z_tile = pl.ds(pl.multiple_of(which * 8, 8), 8)

    @pl.when(own_w)
    def _():
        wait_bytes(wrs.at[pl.ds(0, NR - 1)], one_r.at[3])
        wz[...] = jnp.sum(wrs[0 : NR - 1], axis=0) + wsend[w_chunk(me)]
        for i in range(2):
            to = base + 8 * i

            @pl.when(to != z)
            def _():
                pltpu.make_async_remote_copy(
                    wz.at[pl.ds(8 * i, 8)], zrs.at[lax.rem(z - to + (NZ - 1), NZ)], one_s.at[4 + i], one_r.at[4],
                    device_id={"shard": to}, device_id_type=MESH,
                ).start()

    tick(2 * HELD + 1)
    gather_terms([-(HELD + 1), HELD + 1])

    @pl.when(own_z)
    def _():
        wait_bytes(zrs.at[pl.ds(0, NZ - 1)], one_r.at[4])
        wfin[z_tile, :] = (jnp.sum(zrs[0 : NZ - 1], axis=0) + wz[z_tile, :]) * (1.0 / NR)

        @pl.loop(1, NZ)
        def _(d):
            pltpu.make_async_remote_copy(
                wfin.at[z_tile], wfin.at[z_tile], one_s.at[6], one_r.at[5 + which],
                device_id={"shard": lax.rem(z + d, NZ)}, device_id_type=MESH,
            ).start()

    tick(2 * HELD + 2)

    @pl.when(own_w)
    def _():
        for i in range(2):
            @pl.when(base + 8 * i != z)
            def _():
                wait_bytes(wfin.at[pl.ds(8 * i, 8)], one_r.at[5 + i])

        rf_ref[w_chunk(me)] = wfin[...]

        @pl.loop(1, NR)
        def _(d):
            pltpu.make_async_remote_copy(
                wfin, rf_ref.at[w_chunk(me)], one_s.at[7], one_r.at[7],
                device_id={"rep": lax.rem(me + d, NR)}, device_id_type=MESH,
            ).start()

    tick(2 * HELD + 3)
    gather_terms([-(HELD + 2), HELD + 2])

    @pl.when(own_w)
    def _():
        wait_bytes(wrs.at[pl.ds(0, W_OWNERS - 1)], one_r.at[7])

    @pl.when(jnp.logical_not(own_w))
    def _():
        wait_bytes(wrs.at[pl.ds(0, W_OWNERS)], one_r.at[7])

    o_hi, o_mid, o_low = split3(ot[...])
    lhs = jnp.concatenate([o_hi, o_hi, o_mid, o_mid, o_hi, o_low], axis=0)

    def rebuild(cols):
        h, m, low = split3(rf_ref[:, cols])
        rebuilt = mm(lhs, jnp.concatenate([h, m, h, m, low, h], axis=0), TN)
        avg_ref[:, cols] = rebuilt.astype(BF16)
        acc[:, cols] -= rebuilt

    columns(rebuild)
    tick(14)
    tick(15)
    last = av[block(zat(8)), :].T

    def finish(cols):
        next_ref[0, :, cols] = (acc[:, cols] + mm(last, ball[block(zat(8)), cols], NN)).astype(BF16)

    columns(finish)

    for k in range(8 * PARTS):
        for way in range(2):
            if used(way, k // PARTS, k % PARTS):
                ring(way, k // PARTS, k % PARTS).wait_send()
    wait_bytes(br.at[:, pl.ds(0, (NZ - 1) * TB)], br_s)
    for i in range(len(hops)):
        u_copy(i).wait_send()
    wait_bytes(grecv.at[pl.ds(0, NZ - 1)], one_s.at[2])

    @pl.when(own_p)
    def _():
        wait_bytes(prs.at[pl.ds(0, P_OWNERS - 1)], one_s.at[0])
        wait_bytes(prs.at[pl.ds(0, NR - 1)], one_s.at[1])

    @pl.when(jnp.logical_not(own_p))
    def _():
        wait_bytes(prs.at[pl.ds(0, P_OWNERS)], one_s.at[0])

    @pl.when(own_w)
    def _():
        wait_bytes(wrs.at[pl.ds(0, W_OWNERS - 1)], one_s.at[3])
        for i in range(2):
            @pl.when(base + 8 * i != z)
            def _():
                wait_bytes(wz.at[pl.ds(8 * i, 8)], one_s.at[4 + i])

        wait_bytes(wrs.at[pl.ds(0, NR - 1)], one_s.at[7])

    @pl.when(jnp.logical_not(own_w))
    def _():
        wait_bytes(wrs.at[pl.ds(0, W_OWNERS)], one_s.at[3])

    @pl.when(own_z)
    def _():
        wait_bytes(zrs.at[pl.ds(0, NZ - 1)], one_s.at[6])


def on_device(activations, output_grad, feedback, right_start):
    n_hops = (8 - HELD) + (7 - HELD)
    dma = pltpu.SemaphoreType.DMA
    averaged, feedback_next, right_t = pl.pallas_call(
        kernel,
        out_shape=(
            jax.ShapeDtypeStruct((H, D), BF16),
            jax.ShapeDtypeStruct((1, H, D), BF16),
            jax.ShapeDtypeStruct((K, D), F32),
        ),
        in_specs=[pl.BlockSpec(memory_space=pltpu.HBM)] * 4,
        out_specs=[pl.BlockSpec(memory_space=pltpu.VMEM)] * 3,
        scratch_shapes=[
            pltpu.VMEM((NZ * TB, D), BF16),
            pltpu.VMEM((NZ * TB, H), BF16),
            pltpu.VMEM((H, D), BF16),
            pltpu.VMEM((K, D), F32),
            pltpu.VMEM((H, D), F32),
            pltpu.VMEM((K, NZ * TB), F32),
            pltpu.VMEM((K, H), F32),
            pltpu.VMEM((NR, 8, 128), F32),
            pltpu.VMEM((K, H), F32),
            pltpu.VMEM((8, 128), F32),
            pltpu.VMEM((NZ, 8, 128), F32),
            pltpu.VMEM((K, H), F32),
            pltpu.VMEM((n_hops, K, TB), F32),
            pltpu.VMEM((n_hops, K, TB), F32),
            pltpu.VMEM((K, D), F32),
            pltpu.VMEM((NR, 16, 128), F32),
            pltpu.VMEM((16, 128), F32),
            pltpu.VMEM((NZ, 8, 128), F32),
            pltpu.VMEM((16, 128), F32),
            dma((4,)),
            dma((2, 8, PARTS)),
            dma((2, 8, PARTS)),
            dma,
            dma,
            dma((n_hops,)),
            dma((n_hops,)),
            dma((8,)),
            dma((8,)),
        ],
        compiler_params=pltpu.CompilerParams(
            collective_id=0, has_side_effects=True, vmem_limit_bytes=48 * 2**20
        ),
        cost_estimate=pl.CostEstimate(
            flops=2 * H * NZ * TB * D, bytes_accessed=5_000_000, transcendentals=0
        ),
    )(activations, output_grad, feedback, right_start.T)
    return averaged, feedback_next, right_t.T


def solution(mesh):
    return jax.shard_map(
        on_device,
        mesh=mesh,
        in_specs=(P("rep", None, "shard"), P("rep", "shard", None), P("rep", "shard", None), P()),
        out_specs=(P("shard", None), P("rep", "shard", None), P()),
        check_vma=False,
    )
```

```python
import jax
import jax.numpy as jnp
from jax import lax
from jax.experimental import pallas as pl
from jax.experimental.pallas import tpu as pltpu
from jax.sharding import PartitionSpec as P

MESH = pl.DeviceIdType.MESH
F32, BF16 = jnp.float32, jnp.bfloat16
NZ, NR = 16, 32
TB, D, H, K = 128, 1664, 256, 32
PARTS = 4
ROWS = TB // PARTS
HELD = 4
P_OWNERS = 8
W_OWNERS = 26
AT = (0, 2, 3, 5, 7, 9, 10, 12, 13, 17, 20, 22, 24, 25, 26)
NN = (((1,), (0,)), ((), ()))
NT = (((1,), (1,)), ((), ()))
TN = (((0,), (0,)), ((), ()))


def mm(a, b, dims):
    return lax.dot_general(a, b, dims, preferred_element_type=F32)


def split3(x):
    hi = x.astype(BF16)
    rest = x - hi.astype(F32)
    mid = rest.astype(BF16)
    low = (rest - mid.astype(F32)).astype(BF16)
    return hi, mid, low


def stack3(x):
    return jnp.concatenate(split3(x), axis=0)


def fold3(x):
    n = x.shape[0] // 3
    return x[:n] + (x[n : 2 * n] + x[2 * n :])


def columns(body):
    def step(i, carry):
        body(pl.ds(pl.multiple_of(i * 256, 256), 256))
        return carry

    lax.fori_loop(0, 6, step, 0)
    body(pl.ds(1536, 128))


def inverse_factor(packed):
    lane = lax.broadcasted_iota(jnp.int32, (8, 128), 1)
    sub = lax.broadcasted_iota(jnp.int32, (8, 128), 0)
    rows = []
    for q in range(4):
        g = pltpu.roll(packed, (32 - 32 * q) % 128, 1) if q != 1 else packed
        g = jnp.where((lane >= 32) & (lane < 64), g, 0.0)
        rows.append(g + jnp.where(lane == sub + 8 * q, 1.0, 0.0))
    for k in range(K):
        q, i = k // 8, k % 8
        row = rows[q][i : i + 1, :]
        pivot = row[:, 32 + k : 33 + k]
        inv = lax.rsqrt(pivot)
        inv = inv * (1.5 - 0.5 * pivot * inv * inv)
        row = row * inv
        for t in range(q, 4):
            col = rows[t][:, 32 + k : 33 + k] * inv
            new = rows[t] - col * row
            if t == q:
                new = jnp.where(sub > i, new, jnp.where(sub == i, row, rows[t]))
            rows[t] = new
    return jnp.concatenate(rows, axis=0)[:, 0:K]


def kernel(
    a_ref, b_ref, f_ref, r_ref, avg_ref, next_ref, rf_ref,
    ball, av, fv, rv, acc, br, psend, prs, ptot, gsum, ot,
    usend, urecv, wsend, wrs, wsum,
    lsem, ssem, rsem, u_s, u_r, one_s, one_r,
):
    z = lax.axis_index("shard")
    me = lax.axis_index("rep")

    def zat(off):
        return lax.rem(z + (off + 2 * NZ), NZ)

    def block(owner):
        return pl.ds(pl.multiple_of(owner * TB, TB), TB)

    loads = [
        pltpu.make_async_copy(b_ref.at[0], ball.at[block(z)], lsem.at[0]),
        pltpu.make_async_copy(r_ref, rv, lsem.at[1]),
        pltpu.make_async_copy(f_ref.at[0], fv, lsem.at[2]),
        pltpu.make_async_copy(a_ref.at[0], av, lsem.at[3]),
    ]
    for load in loads:
        load.start()

    barrier = pltpu.get_barrier_semaphore()

    @pl.loop(1, NZ)
    def _(d):
        pl.semaphore_signal(barrier, inc=1, device_id={"shard": lax.rem(z + d, NZ)}, device_id_type=MESH)

    @pl.loop(1, NR)
    def _(d):
        pl.semaphore_signal(barrier, inc=1, device_id={"rep": lax.rem(me + d, NR)}, device_id_type=MESH)

    def wait_bytes(ref, sem):
        pltpu.make_async_copy(ref, ref, sem).wait()

    def piece(owner, part):
        return ball.at[pl.ds(pl.multiple_of(owner * TB + part * ROWS, ROWS), ROWS)]

    def ring(way, s, part):
        owner, to = (zat(-s), zat(1)) if way == 0 else (zat(s), zat(-1))
        source = piece(owner, part) if s else b_ref.at[0, pl.ds(part * ROWS, ROWS)]
        return pltpu.make_async_remote_copy(
            source, piece(owner, part), ssem.at[way, s, part], rsem.at[way, s, part],
            device_id={"shard": to}, device_id_type=MESH,
        )

    def used(way, s, part):
        return s < 7 or (s == 7 and (part < PARTS // 2) == (way == 0))

    done = [0]

    def ticks(upto):
        for k in range(done[0], upto):
            s = k // PARTS
            for way in range(2):
                part = k % PARTS if way == 0 else PARTS - 1 - k % PARTS
                if used(way, s, part):
                    ring(way, s, part).wait_recv()
                    if used(way, s + 1, part):
                        ring(way, s + 1, part).start()
        done[0] = max(done[0], upto)

    def gather_terms(offsets):
        at = jnp.concatenate([av[block(zat(o)), :].T for o in offsets], axis=1)

        def body(cols):
            rows = jnp.concatenate([ball[block(zat(o)), cols] for o in offsets], axis=0)
            acc[:, cols] += mm(at, rows, NN)

        columns(body)

    pl.semaphore_wait(barrier, NZ - 1 + NR - 1)
    for k in range(PARTS):
        for way in range(2):
            ring(way, 0, k if way == 0 else PARTS - 1 - k).start()

    loads[0].wait()
    loads[1].wait()
    r3 = stack3(rv[...])
    br[z] = fold3(mm(r3, ball[block(z), :], NT))

    def br_send(owner, off, i):
        pltpu.make_async_remote_copy(
            br.at[owner], br.at[owner], one_s.at[i], one_r.at[i],
            device_id={"shard": zat(off)}, device_id_type=MESH,
        ).start()

    for off in (6, -6, 3, -3):
        br_send(z, off, 8)
    for off in (1, -1):
        br_send(z, off, 9)

    loads[2].wait()
    fr = fold3(mm(r3, fv[...], NT))
    columns(lambda cols: acc.__setitem__((slice(None), cols), fv[:, cols].astype(F32)))
    loads[3].wait()
    ticks(AT[0])
    wait_bytes(br.at[pl.ds(0, 4)], one_r.at[8])
    for off in (1, -1):
        for o in (3, -3, 6, -6):
            br_send(zat(o), off, 9)
    br_send(zat(-6), 2, 9)
    ticks(AT[1])
    wait_bytes(br.at[pl.ds(0, 11)], one_r.at[9])
    br3 = stack3(jnp.concatenate([br[i] for i in range(NZ)], axis=1))
    psend[...] = fr + fold3(mm(br3, av[...], NN))

    def z_first(ref, i):
        for off in (4, 8, 12):
            pltpu.make_async_remote_copy(
                ref.at[z // 4], ref.at[z // 4], one_s.at[i], one_r.at[i],
                device_id={"shard": zat(off)}, device_id_type=MESH,
            ).start()

    def z_second(ref, i):
        wait_bytes(ref.at[pl.ds(0, 3)], one_r.at[i])
        mine = 4 + lax.rem(z, 4)
        ref[mine] = (ref[0] + ref[1]) + (ref[2] + ref[3])
        for off in (1, 2, -1):
            pltpu.make_async_remote_copy(
                ref.at[mine], ref.at[mine], one_s.at[i + 1], one_r.at[i + 1],
                device_id={"shard": zat(off)}, device_id_type=MESH,
            ).start()

    def z_total(ref, i):
        wait_bytes(ref.at[pl.ds(0, 3)], one_r.at[i + 1])
        return (ref[4] + ref[5]) + (ref[6] + ref[7])

    def p_tile(o):
        return (
            pl.ds(pl.multiple_of(o // 2 * 8, 8), 8),
            pl.ds(pl.multiple_of(o % 2 * 128, 128), 128),
        )

    @pl.loop(0, P_OWNERS)
    def _(o):
        to = 4 * o

        @pl.when(to != me)
        def _():
            pltpu.make_async_remote_copy(
                psend.at[p_tile(o)], prs.at[lax.rem(me - to + (NR - 1), NR)], one_s.at[0], one_r.at[0],
                device_id={"rep": to}, device_id_type=MESH,
            ).start()

    ticks(AT[2])
    gather_terms([0])
    ticks(AT[3])
    own_p = lax.rem(me, 4) == 0

    @pl.when(own_p)
    def _():
        wait_bytes(prs.at[pl.ds(0, NR - 1)], one_r.at[0])
        tile = p_tile(me // 4)
        ptot[tile] = jnp.sum(prs[0 : NR - 1], axis=0) + psend[tile]

        @pl.loop(1, NR)
        def _(d):
            pltpu.make_async_remote_copy(
                ptot.at[tile], ptot.at[tile], one_s.at[1], one_r.at[1],
                device_id={"rep": lax.rem(me + d, NR)}, device_id_type=MESH,
            ).start()

    gather_terms([-1, 1])
    ticks(AT[4])

    @pl.when(own_p)
    def _():
        wait_bytes(prs.at[pl.ds(0, P_OWNERS - 1)], one_r.at[1])

    @pl.when(jnp.logical_not(own_p))
    def _():
        wait_bytes(prs.at[pl.ds(0, P_OWNERS)], one_r.at[1])

    pt = ptot[...]
    p_hi, p_mid, p_low = split3(pt)
    wide = jnp.concatenate([pt] * 4, axis=0)
    w_hi, w_mid, w_low = split3(wide)
    g = mm(p_hi, w_hi, NT) + (
        (mm(p_hi, w_mid, NT) + mm(p_mid, w_hi, NT))
        + (mm(p_mid, w_mid, NT) + mm(p_hi, w_low, NT) + mm(p_low, w_hi, NT))
    )
    lane = lax.broadcasted_iota(jnp.int32, (8, 128), 1)
    packed = jnp.zeros((8, 128), F32)
    for q in range(4):
        packed = jnp.where((lane >= 32 * q) & (lane < 32 * q + 32), g[8 * q : 8 * q + 8], packed)
    gsum[z // 4] = packed
    z_first(gsum, 2)
    ticks(AT[5])
    gather_terms([-2, 2])
    ticks(AT[6])
    z_second(gsum, 2)
    ticks(AT[7])
    l_inv = inverse_factor(z_total(gsum, 2))
    ticks(AT[8])
    l_hi, l_mid, l_low = split3(l_inv)
    o_t = mm(l_hi, p_hi, NN) + (
        (mm(l_hi, p_mid, NN) + mm(l_mid, p_hi, NN))
        + (mm(l_mid, p_mid, NN) + mm(l_hi, p_low, NN) + mm(l_low, p_hi, NN))
    )
    ot[...] = o_t
    o3 = stack3(o_t)

    hops = [(o, o - HELD) for o in range(HELD + 1, 9)] + [(-o, HELD - o) for o in range(HELD + 1, 8)]

    def u_copy(i):
        return pltpu.make_async_remote_copy(
            usend.at[i], urecv.at[i], u_s.at[i], u_r.at[i],
            device_id={"shard": zat(hops[i][1])}, device_id_type=MESH,
        )

    for i, (o, _) in enumerate(hops):
        usend[i] = fold3(mm(o3, av[block(zat(o)), :], NT))
        u_copy(i).start()
    for s in range(3, HELD + 1):
        ticks(PARTS * s)
        gather_terms([-s, s])
    for i in range(len(hops)):
        u_copy(i).wait_recv()
    u_up = sum(urecv[i] for i in range(len(hops)) if hops[i][0] > 0)
    u_down = sum(urecv[i] for i in range(len(hops)) if hops[i][0] < 0)
    u3 = stack3(jnp.concatenate([u_up, u_down], axis=1))

    def w_terms(cols):
        m_hi, m_mid, _ = split3(acc[:, cols])
        rows = jnp.concatenate([ball[block(zat(HELD)), cols], ball[block(zat(-HELD)), cols]], axis=0)
        total = mm(o3, m_hi, NN) + mm(u3, rows, NN)
        cross = mm(o3[: 2 * K], m_mid, NN)
        wsend[:, cols] = fold3(total) + (cross[:K] + cross[K:])

    columns(w_terms)

    def w_chunk(q):
        return (
            pl.ds(pl.multiple_of(lax.rem(q, 2) * 16, 16), 16),
            pl.ds(pl.multiple_of(q // 2 * 128, 128), 128),
        )

    @pl.loop(0, W_OWNERS)
    def _(q):
        @pl.when(q != me)
        def _():
            pltpu.make_async_remote_copy(
                wsend.at[w_chunk(q)], wrs.at[lax.rem(me - q + (NR - 1), NR)], one_s.at[4], one_r.at[4],
                device_id={"rep": q}, device_id_type=MESH,
            ).start()

    ticks(AT[9])
    own_w = me < W_OWNERS

    @pl.when(own_w)
    def _():
        wait_bytes(wrs.at[pl.ds(0, NR - 1)], one_r.at[4])
        wsum[z // 4] = jnp.sum(wrs[0 : NR - 1], axis=0) + wsend[w_chunk(me)]
        z_first(wsum, 5)

    ticks(AT[10])
    gather_terms([-5, 5])
    ticks(AT[11])

    @pl.when(own_w)
    def _():
        z_second(wsum, 5)

    ticks(AT[12])

    @pl.when(own_w)
    def _():
        rf_ref[w_chunk(me)] = z_total(wsum, 5) * (1.0 / NR)

        @pl.loop(1, NR)
        def _(d):
            pltpu.make_async_remote_copy(
                rf_ref.at[w_chunk(me)], rf_ref.at[w_chunk(me)], one_s.at[7], one_r.at[7],
                device_id={"rep": lax.rem(me + d, NR)}, device_id_type=MESH,
            ).start()

    ticks(AT[13])
    gather_terms([-6, 6])
    ticks(AT[14])

    @pl.when(own_w)
    def _():
        wait_bytes(wrs.at[pl.ds(0, W_OWNERS - 1)], one_r.at[7])

    @pl.when(jnp.logical_not(own_w))
    def _():
        wait_bytes(wrs.at[pl.ds(0, W_OWNERS)], one_r.at[7])

    o_hi, o_mid, o_low = split3(ot[...])
    lhs = jnp.concatenate([o_hi, o_hi, o_mid, o_mid, o_hi, o_low], axis=0)

    def rebuild(cols):
        h, m, low = split3(rf_ref[:, cols])
        rebuilt = mm(lhs, jnp.concatenate([h, m, h, m, low, h], axis=0), TN)
        avg_ref[:, cols] = rebuilt.astype(BF16)
        acc[:, cols] -= rebuilt

    columns(rebuild)
    ticks(PARTS * 7)
    gather_terms([-7, 7])
    ticks(PARTS * 8)
    last = av[block(zat(8)), :].T

    def finish(cols):
        next_ref[0, :, cols] = (acc[:, cols] + mm(last, ball[block(zat(8)), cols], NN)).astype(BF16)

    columns(finish)

    for k in range(8 * PARTS):
        for way in range(2):
            if used(way, k // PARTS, k % PARTS):
                ring(way, k // PARTS, k % PARTS).wait_send()
    wait_bytes(br.at[pl.ds(0, 4)], one_s.at[8])
    wait_bytes(br.at[pl.ds(0, 11)], one_s.at[9])
    for i in range(len(hops)):
        u_copy(i).wait_send()
    for i in (2, 3):
        wait_bytes(gsum.at[pl.ds(0, 3)], one_s.at[i])

    @pl.when(own_p)
    def _():
        wait_bytes(prs.at[pl.ds(0, P_OWNERS - 1)], one_s.at[0])
        wait_bytes(prs.at[pl.ds(0, NR - 1)], one_s.at[1])

    @pl.when(jnp.logical_not(own_p))
    def _():
        wait_bytes(prs.at[pl.ds(0, P_OWNERS)], one_s.at[0])

    @pl.when(own_w)
    def _():
        wait_bytes(wrs.at[pl.ds(0, W_OWNERS - 1)], one_s.at[4])
        for i in (5, 6):
            wait_bytes(wsum.at[pl.ds(0, 3)], one_s.at[i])
        wait_bytes(wrs.at[pl.ds(0, NR - 1)], one_s.at[7])

    @pl.when(jnp.logical_not(own_w))
    def _():
        wait_bytes(wrs.at[pl.ds(0, W_OWNERS)], one_s.at[4])


def store(avg_ref, next_ref, rf_ref, avg_out, next_out, rf_out, sem):
    copies = [
        pltpu.make_async_copy(avg_ref, avg_out, sem.at[0]),
        pltpu.make_async_copy(next_ref, next_out, sem.at[1]),
        pltpu.make_async_copy(rf_ref, rf_out, sem.at[2]),
    ]
    for copy in copies:
        copy.start()
    for copy in copies:
        copy.wait()


def on_device(activations, output_grad, feedback, right_start):
    n_hops = (8 - HELD) + (7 - HELD)
    dma = pltpu.SemaphoreType.DMA
    shapes = (
        jax.ShapeDtypeStruct((H, D), BF16),
        jax.ShapeDtypeStruct((1, H, D), BF16),
        jax.ShapeDtypeStruct((K, D), F32),
    )
    results = pl.pallas_call(
        kernel,
        out_shape=tuple(pltpu.VMEM(s.shape, s.dtype) for s in shapes),
        in_specs=[pl.BlockSpec(memory_space=pltpu.HBM)] * 4,
        out_specs=[pl.BlockSpec(memory_space=pltpu.VMEM)] * 3,
        scratch_shapes=[
            pltpu.VMEM((NZ * TB, D), BF16),
            pltpu.VMEM((NZ * TB, H), BF16),
            pltpu.VMEM((H, D), BF16),
            pltpu.VMEM((K, D), F32),
            pltpu.VMEM((H, D), F32),
            pltpu.VMEM((NZ, K, TB), F32),
            pltpu.VMEM((K, H), F32),
            pltpu.VMEM((NR, 8, 128), F32),
            pltpu.VMEM((K, H), F32),
            pltpu.VMEM((8, 8, 128), F32),
            pltpu.VMEM((K, H), F32),
            pltpu.VMEM((n_hops, K, TB), F32),
            pltpu.VMEM((n_hops, K, TB), F32),
            pltpu.VMEM((K, D), F32),
            pltpu.VMEM((NR, 16, 128), F32),
            pltpu.VMEM((8, 16, 128), F32),
            dma((4,)),
            dma((2, 8, PARTS)),
            dma((2, 8, PARTS)),
            dma((n_hops,)),
            dma((n_hops,)),
            dma((10,)),
            dma((10,)),
        ],
        compiler_params=pltpu.CompilerParams(
            collective_id=0, has_side_effects=True, vmem_limit_bytes=61 * 2**20
        ),
        cost_estimate=pl.CostEstimate(
            flops=2 * H * NZ * TB * D, bytes_accessed=5_000_000, transcendentals=0
        ),
    )(activations, output_grad, feedback, right_start.T)
    averaged, feedback_next, right_t = pl.pallas_call(
        store,
        out_shape=shapes,
        in_specs=[pl.BlockSpec(memory_space=pl.ANY)] * 3,
        out_specs=[pl.BlockSpec(memory_space=pltpu.HBM)] * 3,
        scratch_shapes=[dma((3,))],
        compiler_params=pltpu.CompilerParams(vmem_limit_bytes=2**20),
    )(*results)
    return averaged, feedback_next, right_t.T


def solution(mesh):
    return jax.shard_map(
        on_device,
        mesh=mesh,
        in_specs=(P("rep", None, "shard"), P("rep", "shard", None), P("rep", "shard", None), P()),
        out_specs=(P("shard", None), P("rep", "shard", None), P()),
        check_vma=False,
    )
```

```python
import jax
import jax.numpy as jnp
from jax import lax
from jax.experimental import pallas as pl
from jax.experimental.pallas import tpu as pltpu
from jax.sharding import PartitionSpec as P

MESH = pl.DeviceIdType.MESH
F32, BF16 = jnp.float32, jnp.bfloat16
NZ, NR = 16, 32
TB, D, H, K = 128, 1664, 256, 32
PARTS = 4
ROWS = TB // PARTS
HELD = 4
NEAR = (3, -3, 2, -2, 1, -1)
P_OWNERS = 8
W_OWNERS = 26
AT = (1, 2, 4, 6, 8, 11, 14, 16, 22, 25, 27, 30, 32)
NN = (((1,), (0,)), ((), ()))
NT = (((1,), (1,)), ((), ()))
TN = (((0,), (0,)), ((), ()))


def mm(a, b, dims):
    return lax.dot_general(a, b, dims, preferred_element_type=F32)


def split3(x):
    hi = x.astype(BF16)
    rest = x - hi.astype(F32)
    mid = rest.astype(BF16)
    low = (rest - mid.astype(F32)).astype(BF16)
    return hi, mid, low


def stack3(x):
    return jnp.concatenate(split3(x), axis=0)


def fold3(x):
    n = x.shape[0] // 3
    return x[:n] + (x[n : 2 * n] + x[2 * n :])


def columns(body):
    def step(i, carry):
        body(pl.ds(pl.multiple_of(i * 256, 256), 256))
        return carry

    lax.fori_loop(0, 6, step, 0)
    body(pl.ds(1536, 128))


def inverse_factor(packed):
    lane = lax.broadcasted_iota(jnp.int32, (8, 128), 1)
    sub = lax.broadcasted_iota(jnp.int32, (8, 128), 0)
    rows = []
    for q in range(4):
        g = pltpu.roll(packed, (32 - 32 * q) % 128, 1) if q != 1 else packed
        g = jnp.where((lane >= 32) & (lane < 64), g, 0.0)
        rows.append(g + jnp.where(lane == sub + 8 * q, 1.0, 0.0))
    for k in range(K):
        q, i = k // 8, k % 8
        row = rows[q][i : i + 1, :]
        pivot = row[:, 32 + k : 33 + k]
        inv = lax.rsqrt(pivot)
        inv = inv * (1.5 - 0.5 * pivot * inv * inv)
        row = row * inv
        for t in range(q, 4):
            col = rows[t][:, 32 + k : 33 + k] * inv
            new = rows[t] - col * row
            if t == q:
                new = jnp.where(sub > i, new, jnp.where(sub == i, row, rows[t]))
            rows[t] = new
    return jnp.concatenate(rows, axis=0)[:, 0:K]


def kernel(
    a_ref, b_ref, f_ref, r_ref, avg_ref, next_ref, rf_ref,
    ball, av, fv, rv, acc, br, psend, prs, ptot, gsum, ot,
    usend, urecv, wsend, wrs, wsum,
    lsem, ssem, rsem, u_s, u_r, one_s, one_r,
):
    z = lax.axis_index("shard")
    me = lax.axis_index("rep")

    def zat(off):
        return lax.rem(z + (off + 2 * NZ), NZ)

    def block(owner):
        return pl.ds(pl.multiple_of(owner * TB, TB), TB)

    loads = [
        pltpu.make_async_copy(b_ref.at[0], ball.at[block(z)], lsem.at[0]),
        pltpu.make_async_copy(r_ref, rv, lsem.at[1]),
        pltpu.make_async_copy(f_ref.at[0], fv, lsem.at[2]),
        pltpu.make_async_copy(a_ref.at[0], av, lsem.at[3]),
    ]
    for load in loads:
        load.start()

    barrier = pltpu.get_barrier_semaphore()

    for off in NEAR:
        pl.semaphore_signal(barrier, inc=1, device_id={"shard": zat(off)}, device_id_type=MESH)

    @pl.loop(1, NR)
    def _(d):
        pl.semaphore_signal(barrier, inc=1, device_id={"rep": lax.rem(me + d, NR)}, device_id_type=MESH)

    def wait_bytes(ref, sem):
        pltpu.make_async_copy(ref, ref, sem).wait()

    def piece(owner, part):
        return ball.at[pl.ds(pl.multiple_of(owner * TB + part * ROWS, ROWS), ROWS)]

    def ring(way, s, part):
        owner, to = (zat(-s), zat(1)) if way == 0 else (zat(s), zat(-1))
        source = piece(owner, part) if s else b_ref.at[0, pl.ds(part * ROWS, ROWS)]
        return pltpu.make_async_remote_copy(
            source, piece(owner, part), ssem.at[way, s, part], rsem.at[way, s, part],
            device_id={"shard": to}, device_id_type=MESH,
        )

    def used(way, s, part):
        return s < 7 or (s == 7 and (part < PARTS // 2) == (way == 0))

    done = [0]

    def ticks(upto):
        for k in range(done[0] - PARTS, upto - PARTS):
            s = k // PARTS
            for way in range(2):
                if s < 0:
                    ring(way, 0, k + PARTS if way == 0 else -1 - k).start()
                    continue
                part = k % PARTS if way == 0 else PARTS - 1 - k % PARTS
                if used(way, s, part):
                    ring(way, s, part).wait_recv()
                    if used(way, s + 1, part):
                        ring(way, s + 1, part).start()
        done[0] = max(done[0], upto)

    def gather_terms(offsets):
        ticks(PARTS * (max(offsets) + 1) if max(offsets) else 0)
        at = jnp.concatenate([av[block(zat(o)), :].T for o in offsets], axis=1)

        def body(cols):
            rows = jnp.concatenate([ball[block(zat(o)), cols] for o in offsets], axis=0)
            acc[:, cols] += mm(at, rows, NN)

        columns(body)

    pl.semaphore_wait(barrier, len(NEAR) + NR - 1)
    ticks(AT[0])

    loads[0].wait()
    loads[1].wait()
    r3 = stack3(rv[...])
    br[z] = fold3(mm(r3, ball[block(z), :], NT))

    def br_send(owner, off, i):
        pltpu.make_async_remote_copy(
            br.at[owner], br.at[owner], one_s.at[i], one_r.at[i],
            device_id={"shard": zat(off)}, device_id_type=MESH,
        ).start()

    for off in (3, -3):
        br_send(z, off, 8)
    for off in (1, -1):
        br_send(z, off, 9)

    loads[2].wait()
    fr = fold3(mm(r3, fv[...], NT))
    columns(lambda cols: acc.__setitem__((slice(None), cols), fv[:, cols].astype(F32)))
    ticks(AT[1])
    loads[3].wait()
    wait_bytes(br.at[pl.ds(0, 2)], one_r.at[8])
    br_send(zat(-3), 3, 10)
    br_send(zat(3), -3, 10)
    for off in (1, -1):
        for o in (3, -3):
            br_send(zat(o), off, 9)
    ticks(AT[2])
    wait_bytes(br.at[pl.ds(0, 2)], one_r.at[10])
    for off in (1, -1):
        for o in (6, -6):
            br_send(zat(o), off, 9)
    br_send(zat(-6), 2, 9)
    ticks(AT[3])
    wait_bytes(br.at[pl.ds(0, 11)], one_r.at[9])
    br3 = stack3(jnp.concatenate([br[i] for i in range(NZ)], axis=1))
    psend[...] = fr + fold3(mm(br3, av[...], NN))

    def z_first(ref, i):
        for off in (4, 8, 12):
            pltpu.make_async_remote_copy(
                ref.at[z // 4], ref.at[z // 4], one_s.at[i], one_r.at[i],
                device_id={"shard": zat(off)}, device_id_type=MESH,
            ).start()

    def z_second(ref, i):
        wait_bytes(ref.at[pl.ds(0, 3)], one_r.at[i])
        mine = 4 + lax.rem(z, 4)
        ref[mine] = (ref[0] + ref[1]) + (ref[2] + ref[3])
        for off in (1, 2, -1):
            pltpu.make_async_remote_copy(
                ref.at[mine], ref.at[mine], one_s.at[i + 1], one_r.at[i + 1],
                device_id={"shard": zat(off)}, device_id_type=MESH,
            ).start()

    def z_total(ref, i):
        wait_bytes(ref.at[pl.ds(0, 3)], one_r.at[i + 1])
        return (ref[4] + ref[5]) + (ref[6] + ref[7])

    def p_tile(o):
        return (
            pl.ds(pl.multiple_of(o // 2 * 8, 8), 8),
            pl.ds(pl.multiple_of(o % 2 * 128, 128), 128),
        )

    @pl.loop(0, P_OWNERS)
    def _(o):
        to = 4 * o

        @pl.when(to != me)
        def _():
            pltpu.make_async_remote_copy(
                psend.at[p_tile(o)], prs.at[lax.rem(me - to + (NR - 1), NR)], one_s.at[0], one_r.at[0],
                device_id={"rep": to}, device_id_type=MESH,
            ).start()

    ticks(AT[4])
    gather_terms([0])
    own_p = lax.rem(me, 4) == 0

    @pl.when(own_p)
    def _():
        wait_bytes(prs.at[pl.ds(0, NR - 1)], one_r.at[0])
        tile = p_tile(me // 4)
        ptot[tile] = jnp.sum(prs[0 : NR - 1], axis=0) + psend[tile]

        @pl.loop(1, NR)
        def _(d):
            pltpu.make_async_remote_copy(
                ptot.at[tile], ptot.at[tile], one_s.at[1], one_r.at[1],
                device_id={"rep": lax.rem(me + d, NR)}, device_id_type=MESH,
            ).start()

    ticks(AT[5])
    gather_terms([-1, 1])

    @pl.when(own_p)
    def _():
        wait_bytes(prs.at[pl.ds(0, P_OWNERS - 1)], one_r.at[1])

    @pl.when(jnp.logical_not(own_p))
    def _():
        wait_bytes(prs.at[pl.ds(0, P_OWNERS)], one_r.at[1])

    pt = ptot[...]
    p_hi, p_mid, p_low = split3(pt)
    wide = jnp.concatenate([pt] * 4, axis=0)
    w_hi, w_mid, w_low = split3(wide)
    g = mm(p_hi, w_hi, NT) + (
        (mm(p_hi, w_mid, NT) + mm(p_mid, w_hi, NT))
        + (mm(p_mid, w_mid, NT) + mm(p_hi, w_low, NT) + mm(p_low, w_hi, NT))
    )
    lane = lax.broadcasted_iota(jnp.int32, (8, 128), 1)
    packed = jnp.zeros((8, 128), F32)
    for q in range(4):
        packed = jnp.where((lane >= 32 * q) & (lane < 32 * q + 32), g[8 * q : 8 * q + 8], packed)
    gsum[z] = packed
    for off in (8, 7, 9, 6, 10, 5, 11, 4, 12, 3, 13, 2, 14, 1, 15):
        pltpu.make_async_remote_copy(
            gsum.at[z], gsum.at[z], one_s.at[2], one_r.at[2],
            device_id={"shard": zat(off)}, device_id_type=MESH,
        ).start()
    ticks(AT[6])
    gather_terms([-2, 2])
    ticks(AT[7])
    wait_bytes(gsum.at[pl.ds(0, NZ - 1)], one_r.at[2])
    l_inv = inverse_factor(jnp.sum(gsum[...], axis=0))
    l_hi, l_mid, l_low = split3(l_inv)
    o_t = mm(l_hi, p_hi, NN) + (
        (mm(l_hi, p_mid, NN) + mm(l_mid, p_hi, NN))
        + (mm(l_mid, p_mid, NN) + mm(l_hi, p_low, NN) + mm(l_low, p_hi, NN))
    )
    ot[...] = o_t
    o3 = stack3(o_t)

    hops = [(o, o - HELD) for o in range(HELD + 1, 9)] + [(-o, HELD - o) for o in range(HELD + 1, 8)]

    def u_copy(i):
        return pltpu.make_async_remote_copy(
            usend.at[i], urecv.at[i], u_s.at[i], u_r.at[i],
            device_id={"shard": zat(hops[i][1])}, device_id_type=MESH,
        )

    for i, (o, _) in enumerate(hops):
        usend[i] = fold3(mm(o3, av[block(zat(o)), :], NT))
        u_copy(i).start()
    for s in range(3, HELD + 1):
        gather_terms([-s, s])
    def held_terms(cols):
        m_hi, m_mid, _ = split3(acc[:, cols])
        cross = mm(o3[: 2 * K], m_mid, NN)
        wsend[:, cols] = fold3(mm(o3, m_hi, NN)) + (cross[:K] + cross[K:])

    columns(held_terms)
    for i in range(len(hops)):
        u_copy(i).wait_recv()
    u_up = sum(urecv[i] for i in range(len(hops)) if hops[i][0] > 0)
    u_down = sum(urecv[i] for i in range(len(hops)) if hops[i][0] < 0)
    u3 = stack3(jnp.concatenate([u_up, u_down], axis=1))

    def w_chunk(q):
        return (
            pl.ds(pl.multiple_of(lax.rem(q, 2) * 16, 16), 16),
            pl.ds(pl.multiple_of(q // 2 * 128, 128), 128),
        )

    def w_terms(i, width):
        cols = pl.ds(pl.multiple_of(i * 256, 256), width)
        rows = jnp.concatenate([ball[block(zat(HELD)), cols], ball[block(zat(-HELD)), cols]], axis=0)
        wsend[:, cols] += fold3(mm(u3, rows, NN))
        for j in range(width // 64):
            q = 4 * i + j

            @pl.when(q != me)
            def _():
                pltpu.make_async_remote_copy(
                    wsend.at[w_chunk(q)], wrs.at[lax.rem(me - q + (NR - 1), NR)], one_s.at[4], one_r.at[4],
                    device_id={"rep": q}, device_id_type=MESH,
                ).start()

    @pl.loop(0, 6)
    def _(i):
        w_terms(i, 256)

    w_terms(6, 128)
    ticks(AT[8])
    own_w = me < W_OWNERS

    @pl.when(own_w)
    def _():
        wait_bytes(wrs.at[pl.ds(0, NR - 1)], one_r.at[4])
        wsum[z // 4] = jnp.sum(wrs[0 : NR - 1], axis=0) + wsend[w_chunk(me)]
        z_first(wsum, 5)

    ticks(AT[9])
    gather_terms([-5, 5])

    @pl.when(own_w)
    def _():
        z_second(wsum, 5)

    ticks(AT[10])

    @pl.when(own_w)
    def _():
        rf_ref[w_chunk(me)] = z_total(wsum, 5) * (1.0 / NR)

        @pl.loop(1, NR)
        def _(d):
            pltpu.make_async_remote_copy(
                rf_ref.at[w_chunk(me)], rf_ref.at[w_chunk(me)], one_s.at[7], one_r.at[7],
                device_id={"rep": lax.rem(me + d, NR)}, device_id_type=MESH,
            ).start()

    ticks(AT[11])
    gather_terms([-6, 6])
    ticks(AT[12])

    @pl.when(own_w)
    def _():
        wait_bytes(wrs.at[pl.ds(0, W_OWNERS - 1)], one_r.at[7])

    @pl.when(jnp.logical_not(own_w))
    def _():
        wait_bytes(wrs.at[pl.ds(0, W_OWNERS)], one_r.at[7])

    o_hi, o_mid, o_low = split3(ot[...])
    lhs = jnp.concatenate([o_hi, o_hi, o_mid, o_mid, o_hi, o_low], axis=0)

    def rebuild(cols):
        h, m, low = split3(rf_ref[:, cols])
        rebuilt = mm(lhs, jnp.concatenate([h, m, h, m, low, h], axis=0), TN)
        avg_ref[:, cols] = rebuilt.astype(BF16)
        acc[:, cols] -= rebuilt

    columns(rebuild)
    gather_terms([-7, 7])
    ticks(PARTS * 9)
    last = av[block(zat(8)), :].T

    def finish(cols):
        next_ref[0, :, cols] = (acc[:, cols] + mm(last, ball[block(zat(8)), cols], NN)).astype(BF16)

    columns(finish)

    for k in range(8 * PARTS):
        for way in range(2):
            if used(way, k // PARTS, k % PARTS):
                ring(way, k // PARTS, k % PARTS).wait_send()
    wait_bytes(br.at[pl.ds(0, 2)], one_s.at[8])
    wait_bytes(br.at[pl.ds(0, 2)], one_s.at[10])
    wait_bytes(br.at[pl.ds(0, 11)], one_s.at[9])
    for i in range(len(hops)):
        u_copy(i).wait_send()
    wait_bytes(gsum.at[pl.ds(0, NZ - 1)], one_s.at[2])

    @pl.when(own_p)
    def _():
        wait_bytes(prs.at[pl.ds(0, P_OWNERS - 1)], one_s.at[0])
        wait_bytes(prs.at[pl.ds(0, NR - 1)], one_s.at[1])

    @pl.when(jnp.logical_not(own_p))
    def _():
        wait_bytes(prs.at[pl.ds(0, P_OWNERS)], one_s.at[0])

    @pl.when(own_w)
    def _():
        wait_bytes(wrs.at[pl.ds(0, W_OWNERS - 1)], one_s.at[4])
        for i in (5, 6):
            wait_bytes(wsum.at[pl.ds(0, 3)], one_s.at[i])
        wait_bytes(wrs.at[pl.ds(0, NR - 1)], one_s.at[7])

    @pl.when(jnp.logical_not(own_w))
    def _():
        wait_bytes(wrs.at[pl.ds(0, W_OWNERS)], one_s.at[4])


def store(avg_ref, next_ref, rf_ref, avg_out, next_out, rf_out, sem):
    copies = [
        pltpu.make_async_copy(avg_ref, avg_out, sem.at[0]),
        pltpu.make_async_copy(next_ref, next_out, sem.at[1]),
        pltpu.make_async_copy(rf_ref, rf_out, sem.at[2]),
    ]
    for copy in copies:
        copy.start()
    for copy in copies:
        copy.wait()


def on_device(activations, output_grad, feedback, right_start):
    n_hops = (8 - HELD) + (7 - HELD)
    dma = pltpu.SemaphoreType.DMA
    shapes = (
        jax.ShapeDtypeStruct((H, D), BF16),
        jax.ShapeDtypeStruct((1, H, D), BF16),
        jax.ShapeDtypeStruct((K, D), F32),
    )
    results = pl.pallas_call(
        kernel,
        out_shape=tuple(pltpu.VMEM(s.shape, s.dtype) for s in shapes),
        in_specs=[pl.BlockSpec(memory_space=pltpu.HBM)] * 4,
        out_specs=[pl.BlockSpec(memory_space=pltpu.VMEM)] * 3,
        scratch_shapes=[
            pltpu.VMEM((NZ * TB, D), BF16),
            pltpu.VMEM((NZ * TB, H), BF16),
            pltpu.VMEM((H, D), BF16),
            pltpu.VMEM((K, D), F32),
            pltpu.VMEM((H, D), F32),
            pltpu.VMEM((NZ, K, TB), F32),
            pltpu.VMEM((K, H), F32),
            pltpu.VMEM((NR, 8, 128), F32),
            pltpu.VMEM((K, H), F32),
            pltpu.VMEM((NZ, 8, 128), F32),
            pltpu.VMEM((K, H), F32),
            pltpu.VMEM((n_hops, K, TB), F32),
            pltpu.VMEM((n_hops, K, TB), F32),
            pltpu.VMEM((K, D), F32),
            pltpu.VMEM((NR, 16, 128), F32),
            pltpu.VMEM((8, 16, 128), F32),
            dma((4,)),
            dma((2, 8, PARTS)),
            dma((2, 8, PARTS)),
            dma((n_hops,)),
            dma((n_hops,)),
            dma((11,)),
            dma((11,)),
        ],
        compiler_params=pltpu.CompilerParams(
            collective_id=0, has_side_effects=True, vmem_limit_bytes=61 * 2**20
        ),
        cost_estimate=pl.CostEstimate(
            flops=2 * H * NZ * TB * D, bytes_accessed=5_000_000, transcendentals=0
        ),
    )(activations, output_grad, feedback, right_start.T)
    averaged, feedback_next, right_t = pl.pallas_call(
        store,
        out_shape=shapes,
        in_specs=[pl.BlockSpec(memory_space=pl.ANY)] * 3,
        out_specs=[pl.BlockSpec(memory_space=pltpu.HBM)] * 3,
        scratch_shapes=[dma((3,))],
        compiler_params=pltpu.CompilerParams(vmem_limit_bytes=2**20),
    )(*results)
    return averaged, feedback_next, right_t.T


def solution(mesh):
    return jax.shard_map(
        on_device,
        mesh=mesh,
        in_specs=(P("rep", None, "shard"), P("rep", "shard", None), P("rep", "shard", None), P()),
        out_specs=(P("shard", None), P("rep", "shard", None), P()),
        check_vma=False,
    )
```

```python
import jax
import jax.numpy as jnp
from jax import lax
from jax.experimental import pallas as pl
from jax.experimental.pallas import tpu as pltpu
from jax.sharding import PartitionSpec as P

MESH = pl.DeviceIdType.MESH
F32, BF16 = jnp.float32, jnp.bfloat16
NZ, NR = 16, 32
TB, D, H, K = 128, 1664, 256, 32
PARTS = 4
ROWS = TB // PARTS
HELD = 4
NEAR = (3, -3, 2, -2, 1, -1)
P_OWNERS = 8
W_OWNERS = 26
AT = (1, 2, 3, 5, 7, 10, 13, 16, 21, 24, 26, 29, 31)
NN = (((1,), (0,)), ((), ()))
NT = (((1,), (1,)), ((), ()))
TN = (((0,), (0,)), ((), ()))


def mm(a, b, dims):
    return lax.dot_general(a, b, dims, preferred_element_type=F32)


def split3(x):
    hi = x.astype(BF16)
    rest = x - hi.astype(F32)
    mid = rest.astype(BF16)
    low = (rest - mid.astype(F32)).astype(BF16)
    return hi, mid, low


def stack3(x):
    return jnp.concatenate(split3(x), axis=0)


def fold3(x):
    n = x.shape[0] // 3
    return x[:n] + (x[n : 2 * n] + x[2 * n :])


def columns(body):
    def step(i, carry):
        body(pl.ds(pl.multiple_of(i * 256, 256), 256))
        return carry

    lax.fori_loop(0, 6, step, 0)
    body(pl.ds(1536, 128))


def inverse_factor(packed):
    lane = lax.broadcasted_iota(jnp.int32, (8, 128), 1)
    sub = lax.broadcasted_iota(jnp.int32, (8, 128), 0)
    rows = []
    for q in range(4):
        g = pltpu.roll(packed, (32 - 32 * q) % 128, 1) if q != 1 else packed
        g = jnp.where((lane >= 32) & (lane < 64), g, 0.0)
        rows.append(g + jnp.where(lane == sub + 8 * q, 1.0, 0.0))
    for k in range(K):
        q, i = k // 8, k % 8
        row = rows[q][i : i + 1, :]
        pivot = row[:, 32 + k : 33 + k]
        inv = lax.rsqrt(pivot)
        inv = inv * (1.5 - 0.5 * pivot * inv * inv)
        row = row * inv
        for t in range(q, 4):
            col = rows[t][:, 32 + k : 33 + k] * inv
            new = rows[t] - col * row
            if t == q:
                new = jnp.where(sub > i, new, jnp.where(sub == i, row, rows[t]))
            rows[t] = new
    return jnp.concatenate(rows, axis=0)[:, 0:K]


def kernel(
    a_ref, b_ref, f_ref, r_ref, avg_ref, next_ref, rf_ref,
    ball, av, fv, rv, acc, br, psend, prs, ptot, gsum, ot,
    usend, urecv, wsend, wrs, wsum,
    lsem, ssem, rsem, u_s, u_r, one_s, one_r,
):
    z = lax.axis_index("shard")
    me = lax.axis_index("rep")

    def zat(off):
        return lax.rem(z + (off + 2 * NZ), NZ)

    def block(owner):
        return pl.ds(pl.multiple_of(owner * TB, TB), TB)

    loads = [
        pltpu.make_async_copy(b_ref.at[0], ball.at[block(z)], lsem.at[0]),
        pltpu.make_async_copy(r_ref, rv, lsem.at[1]),
        pltpu.make_async_copy(f_ref.at[0], fv, lsem.at[2]),
        pltpu.make_async_copy(a_ref.at[0], av, lsem.at[3]),
    ]
    for load in loads:
        load.start()

    barrier = pltpu.get_barrier_semaphore()

    for off in NEAR:
        pl.semaphore_signal(barrier, inc=1, device_id={"shard": zat(off)}, device_id_type=MESH)

    @pl.loop(1, NR)
    def _(d):
        pl.semaphore_signal(barrier, inc=1, device_id={"rep": lax.rem(me + d, NR)}, device_id_type=MESH)

    def wait_bytes(ref, sem):
        pltpu.make_async_copy(ref, ref, sem).wait()

    def piece(owner, part):
        return ball.at[pl.ds(pl.multiple_of(owner * TB + part * ROWS, ROWS), ROWS)]

    def ring(way, s, part):
        owner, to = (zat(-s), zat(1)) if way == 0 else (zat(s), zat(-1))
        source = piece(owner, part) if s else b_ref.at[0, pl.ds(part * ROWS, ROWS)]
        return pltpu.make_async_remote_copy(
            source, piece(owner, part), ssem.at[way, s, part], rsem.at[way, s, part],
            device_id={"shard": to}, device_id_type=MESH,
        )

    def used(way, s, part):
        return s < 7 or (s == 7 and (part < PARTS // 2) == (way == 0))

    done = [0]

    def ticks(upto):
        for k in range(done[0] - PARTS, upto - PARTS):
            s = k // PARTS
            for way in range(2):
                if s < 0:
                    ring(way, 0, k + PARTS if way == 0 else -1 - k).start()
                    continue
                part = k % PARTS if way == 0 else PARTS - 1 - k % PARTS
                if used(way, s, part):
                    ring(way, s, part).wait_recv()
                    if used(way, s + 1, part):
                        ring(way, s + 1, part).start()
        done[0] = max(done[0], upto)

    def gather_terms(offsets):
        ticks(PARTS * (max(offsets) + 1) if max(offsets) else 0)
        at = jnp.concatenate([av[block(zat(o)), :].T for o in offsets], axis=1)

        def body(cols):
            rows = jnp.concatenate([ball[block(zat(o)), cols] for o in offsets], axis=0)
            acc[:, cols] += mm(at, rows, NN)

        columns(body)

    pl.semaphore_wait(barrier, len(NEAR) + NR - 1)
    ticks(AT[0])

    loads[0].wait()
    loads[1].wait()
    r3 = stack3(rv[...])
    br[z] = fold3(mm(r3, ball[block(z), :], NT))

    def br_send(owner, off, i):
        pltpu.make_async_remote_copy(
            br.at[owner], br.at[owner], one_s.at[i], one_r.at[i],
            device_id={"shard": zat(off)}, device_id_type=MESH,
        ).start()

    for off in (3, -3):
        br_send(z, off, 8)
    for off in (1, -1):
        br_send(z, off, 9)

    loads[2].wait()
    fr = fold3(mm(r3, fv[...], NT))
    columns(lambda cols: acc.__setitem__((slice(None), cols), fv[:, cols].astype(F32)))
    ticks(AT[1])
    loads[3].wait()
    wait_bytes(br.at[pl.ds(0, 2)], one_r.at[8])
    br_send(zat(-3), 3, 10)
    br_send(zat(3), -3, 10)
    for off in (1, -1):
        for o in (3, -3):
            br_send(zat(o), off, 9)
    ticks(AT[2])
    wait_bytes(br.at[pl.ds(0, 2)], one_r.at[10])
    for off in (1, -1):
        for o in (6, -6):
            br_send(zat(o), off, 9)
    br_send(zat(-6), 2, 9)
    ticks(AT[3])
    wait_bytes(br.at[pl.ds(0, 11)], one_r.at[9])
    br3 = stack3(jnp.concatenate([br[i] for i in range(NZ)], axis=1))
    psend[...] = fr + fold3(mm(br3, av[...], NN))

    def z_first(ref, i):
        for off in (4, 8, 12):
            pltpu.make_async_remote_copy(
                ref.at[z // 4], ref.at[z // 4], one_s.at[i], one_r.at[i],
                device_id={"shard": zat(off)}, device_id_type=MESH,
            ).start()

    def z_second(ref, i):
        wait_bytes(ref.at[pl.ds(0, 3)], one_r.at[i])
        mine = 4 + lax.rem(z, 4)
        ref[mine] = (ref[0] + ref[1]) + (ref[2] + ref[3])
        for off in (1, 2, -1):
            pltpu.make_async_remote_copy(
                ref.at[mine], ref.at[mine], one_s.at[i + 1], one_r.at[i + 1],
                device_id={"shard": zat(off)}, device_id_type=MESH,
            ).start()

    def z_total(ref, i):
        wait_bytes(ref.at[pl.ds(0, 3)], one_r.at[i + 1])
        return (ref[4] + ref[5]) + (ref[6] + ref[7])

    def p_tile(o):
        return (
            pl.ds(pl.multiple_of(o // 2 * 8, 8), 8),
            pl.ds(pl.multiple_of(o % 2 * 128, 128), 128),
        )

    @pl.loop(0, P_OWNERS)
    def _(o):
        to = 4 * o

        @pl.when(to != me)
        def _():
            pltpu.make_async_remote_copy(
                psend.at[p_tile(o)], prs.at[lax.rem(me - to + (NR - 1), NR)], one_s.at[0], one_r.at[0],
                device_id={"rep": to}, device_id_type=MESH,
            ).start()

    ticks(AT[4])
    gather_terms([0])
    own_p = lax.rem(me, 4) == 0

    @pl.when(own_p)
    def _():
        wait_bytes(prs.at[pl.ds(0, NR - 1)], one_r.at[0])
        tile = p_tile(me // 4)
        ptot[tile] = jnp.sum(prs[0 : NR - 1], axis=0) + psend[tile]

        @pl.loop(1, NR)
        def _(d):
            pltpu.make_async_remote_copy(
                ptot.at[tile], ptot.at[tile], one_s.at[1], one_r.at[1],
                device_id={"rep": lax.rem(me + d, NR)}, device_id_type=MESH,
            ).start()

    ticks(AT[5])
    gather_terms([-1, 1])

    @pl.when(own_p)
    def _():
        wait_bytes(prs.at[pl.ds(0, P_OWNERS - 1)], one_r.at[1])

    @pl.when(jnp.logical_not(own_p))
    def _():
        wait_bytes(prs.at[pl.ds(0, P_OWNERS)], one_r.at[1])

    pt = ptot[...]
    p_hi, p_mid, p_low = split3(pt)
    wide = jnp.concatenate([pt] * 4, axis=0)
    w_hi, w_mid, w_low = split3(wide)
    g = mm(p_hi, w_hi, NT) + (
        (mm(p_hi, w_mid, NT) + mm(p_mid, w_hi, NT))
        + (mm(p_mid, w_mid, NT) + mm(p_hi, w_low, NT) + mm(p_low, w_hi, NT))
    )
    lane = lax.broadcasted_iota(jnp.int32, (8, 128), 1)
    packed = jnp.zeros((8, 128), F32)
    for q in range(4):
        packed = jnp.where((lane >= 32 * q) & (lane < 32 * q + 32), g[8 * q : 8 * q + 8], packed)
    gsum[z // 4] = packed
    z_first(gsum, 2)
    ticks(AT[6])
    gather_terms([-2, 2])
    z_second(gsum, 2)
    ticks(AT[7])
    l_inv = inverse_factor(z_total(gsum, 2))
    l_hi, l_mid, l_low = split3(l_inv)
    o_t = mm(l_hi, p_hi, NN) + (
        (mm(l_hi, p_mid, NN) + mm(l_mid, p_hi, NN))
        + (mm(l_mid, p_mid, NN) + mm(l_hi, p_low, NN) + mm(l_low, p_hi, NN))
    )
    ot[...] = o_t
    o3 = stack3(o_t)

    hops = [(o, o - HELD) for o in range(HELD + 1, 9)] + [(-o, HELD - o) for o in range(HELD + 1, 8)]

    def u_copy(i):
        return pltpu.make_async_remote_copy(
            usend.at[i], urecv.at[i], u_s.at[i], u_r.at[i],
            device_id={"shard": zat(hops[i][1])}, device_id_type=MESH,
        )

    for i, (o, _) in enumerate(hops):
        usend[i] = fold3(mm(o3, av[block(zat(o)), :], NT))
        u_copy(i).start()
    for s in range(3, HELD + 1):
        gather_terms([-s, s])
    def held_terms(cols):
        m_hi, m_mid, _ = split3(acc[:, cols])
        cross = mm(o3[: 2 * K], m_mid, NN)
        wsend[:, cols] = fold3(mm(o3, m_hi, NN)) + (cross[:K] + cross[K:])

    columns(held_terms)
    for i in range(len(hops)):
        u_copy(i).wait_recv()
    u_up = sum(urecv[i] for i in range(len(hops)) if hops[i][0] > 0)
    u_down = sum(urecv[i] for i in range(len(hops)) if hops[i][0] < 0)
    u3 = stack3(jnp.concatenate([u_up, u_down], axis=1))

    def w_chunk(q):
        return (
            pl.ds(pl.multiple_of(lax.rem(q, 2) * 16, 16), 16),
            pl.ds(pl.multiple_of(q // 2 * 128, 128), 128),
        )

    def w_terms(i, width):
        cols = pl.ds(pl.multiple_of(i * 256, 256), width)
        rows = jnp.concatenate([ball[block(zat(HELD)), cols], ball[block(zat(-HELD)), cols]], axis=0)
        wsend[:, cols] += fold3(mm(u3, rows, NN))
        for j in range(width // 64):
            q = 4 * i + j

            @pl.when(q != me)
            def _():
                pltpu.make_async_remote_copy(
                    wsend.at[w_chunk(q)], wrs.at[lax.rem(me - q + (NR - 1), NR)], one_s.at[4], one_r.at[4],
                    device_id={"rep": q}, device_id_type=MESH,
                ).start()

    @pl.loop(0, 6)
    def _(i):
        w_terms(i, 256)

    w_terms(6, 128)
    ticks(AT[8])
    own_w = me < W_OWNERS

    @pl.when(own_w)
    def _():
        wait_bytes(wrs.at[pl.ds(0, NR - 1)], one_r.at[4])
        wsum[z // 4] = jnp.sum(wrs[0 : NR - 1], axis=0) + wsend[w_chunk(me)]
        z_first(wsum, 5)

    ticks(AT[9])
    gather_terms([-5, 5])

    @pl.when(own_w)
    def _():
        z_second(wsum, 5)

    ticks(AT[10])

    @pl.when(own_w)
    def _():
        rf_ref[w_chunk(me)] = z_total(wsum, 5) * (1.0 / NR)

        @pl.loop(1, NR)
        def _(d):
            pltpu.make_async_remote_copy(
                rf_ref.at[w_chunk(me)], rf_ref.at[w_chunk(me)], one_s.at[7], one_r.at[7],
                device_id={"rep": lax.rem(me + d, NR)}, device_id_type=MESH,
            ).start()

    ticks(AT[11])
    gather_terms([-6, 6])
    ticks(AT[12])

    @pl.when(own_w)
    def _():
        wait_bytes(wrs.at[pl.ds(0, W_OWNERS - 1)], one_r.at[7])

    @pl.when(jnp.logical_not(own_w))
    def _():
        wait_bytes(wrs.at[pl.ds(0, W_OWNERS)], one_r.at[7])

    o_hi, o_mid, o_low = split3(ot[...])
    lhs = jnp.concatenate([o_hi, o_hi, o_mid, o_mid, o_hi, o_low], axis=0)

    def rebuild(cols):
        h, m, low = split3(rf_ref[:, cols])
        rebuilt = mm(lhs, jnp.concatenate([h, m, h, m, low, h], axis=0), TN)
        avg_ref[:, cols] = rebuilt.astype(BF16)
        acc[:, cols] -= rebuilt

    columns(rebuild)
    gather_terms([-7, 7])
    ticks(PARTS * 9)
    last = av[block(zat(8)), :].T

    def finish(cols):
        next_ref[0, :, cols] = (acc[:, cols] + mm(last, ball[block(zat(8)), cols], NN)).astype(BF16)

    columns(finish)

    for k in range(8 * PARTS):
        for way in range(2):
            if used(way, k // PARTS, k % PARTS):
                ring(way, k // PARTS, k % PARTS).wait_send()
    wait_bytes(br.at[pl.ds(0, 2)], one_s.at[8])
    wait_bytes(br.at[pl.ds(0, 2)], one_s.at[10])
    wait_bytes(br.at[pl.ds(0, 11)], one_s.at[9])
    for i in range(len(hops)):
        u_copy(i).wait_send()
    for i in (2, 3):
        wait_bytes(gsum.at[pl.ds(0, 3)], one_s.at[i])

    @pl.when(own_p)
    def _():
        wait_bytes(prs.at[pl.ds(0, P_OWNERS - 1)], one_s.at[0])
        wait_bytes(prs.at[pl.ds(0, NR - 1)], one_s.at[1])

    @pl.when(jnp.logical_not(own_p))
    def _():
        wait_bytes(prs.at[pl.ds(0, P_OWNERS)], one_s.at[0])

    @pl.when(own_w)
    def _():
        wait_bytes(wrs.at[pl.ds(0, W_OWNERS - 1)], one_s.at[4])
        for i in (5, 6):
            wait_bytes(wsum.at[pl.ds(0, 3)], one_s.at[i])
        wait_bytes(wrs.at[pl.ds(0, NR - 1)], one_s.at[7])

    @pl.when(jnp.logical_not(own_w))
    def _():
        wait_bytes(wrs.at[pl.ds(0, W_OWNERS)], one_s.at[4])


def store(avg_ref, next_ref, rf_ref, avg_out, next_out, rf_out, sem):
    copies = [
        pltpu.make_async_copy(avg_ref, avg_out, sem.at[0]),
        pltpu.make_async_copy(next_ref, next_out, sem.at[1]),
        pltpu.make_async_copy(rf_ref, rf_out, sem.at[2]),
    ]
    for copy in copies:
        copy.start()
    for copy in copies:
        copy.wait()


def on_device(activations, output_grad, feedback, right_start):
    n_hops = (8 - HELD) + (7 - HELD)
    dma = pltpu.SemaphoreType.DMA
    shapes = (
        jax.ShapeDtypeStruct((H, D), BF16),
        jax.ShapeDtypeStruct((1, H, D), BF16),
        jax.ShapeDtypeStruct((K, D), F32),
    )
    results = pl.pallas_call(
        kernel,
        out_shape=tuple(pltpu.VMEM(s.shape, s.dtype) for s in shapes),
        in_specs=[pl.BlockSpec(memory_space=pltpu.HBM)] * 4,
        out_specs=[pl.BlockSpec(memory_space=pltpu.VMEM)] * 3,
        scratch_shapes=[
            pltpu.VMEM((NZ * TB, D), BF16),
            pltpu.VMEM((NZ * TB, H), BF16),
            pltpu.VMEM((H, D), BF16),
            pltpu.VMEM((K, D), F32),
            pltpu.VMEM((H, D), F32),
            pltpu.VMEM((NZ, K, TB), F32),
            pltpu.VMEM((K, H), F32),
            pltpu.VMEM((NR, 8, 128), F32),
            pltpu.VMEM((K, H), F32),
            pltpu.VMEM((8, 8, 128), F32),
            pltpu.VMEM((K, H), F32),
            pltpu.VMEM((n_hops, K, TB), F32),
            pltpu.VMEM((n_hops, K, TB), F32),
            pltpu.VMEM((K, D), F32),
            pltpu.VMEM((NR, 16, 128), F32),
            pltpu.VMEM((8, 16, 128), F32),
            dma((4,)),
            dma((2, 8, PARTS)),
            dma((2, 8, PARTS)),
            dma((n_hops,)),
            dma((n_hops,)),
            dma((11,)),
            dma((11,)),
        ],
        compiler_params=pltpu.CompilerParams(
            collective_id=0, has_side_effects=True, vmem_limit_bytes=61 * 2**20
        ),
        cost_estimate=pl.CostEstimate(
            flops=2 * H * NZ * TB * D, bytes_accessed=5_000_000, transcendentals=0
        ),
    )(activations, output_grad, feedback, right_start.T)
    averaged, feedback_next, right_t = pl.pallas_call(
        store,
        out_shape=shapes,
        in_specs=[pl.BlockSpec(memory_space=pl.ANY)] * 3,
        out_specs=[pl.BlockSpec(memory_space=pltpu.HBM)] * 3,
        scratch_shapes=[dma((3,))],
        compiler_params=pltpu.CompilerParams(vmem_limit_bytes=2**20),
    )(*results)
    return averaged, feedback_next, right_t.T


def solution(mesh):
    return jax.shard_map(
        on_device,
        mesh=mesh,
        in_specs=(P("rep", None, "shard"), P("rep", "shard", None), P("rep", "shard", None), P()),
        out_specs=(P("shard", None), P("rep", "shard", None), P()),
        check_vma=False,
    )
```

```python
import jax
import jax.numpy as jnp
from jax import lax
from jax.experimental import pallas as pl
from jax.experimental.pallas import tpu as pltpu
from jax.sharding import PartitionSpec as P

MESH = pl.DeviceIdType.MESH
F32, BF16 = jnp.float32, jnp.bfloat16
NZ, NR = 16, 32
TB, D, H, K = 128, 1664, 256, 32
PARTS = 4
ROWS = TB // PARTS
HELD = 4
NEAR = (3, -3, 2, -2, 1, -1)
P_OWNERS = 8
W_OWNERS = 26
AT = (1, 2, 3, 5, 7, 10, 13, 16, 21, 24, 26, 29, 31)
NN = (((1,), (0,)), ((), ()))
NT = (((1,), (1,)), ((), ()))
TN = (((0,), (0,)), ((), ()))


def mm(a, b, dims):
    return lax.dot_general(a, b, dims, preferred_element_type=F32)


def split3(x):
    hi = x.astype(BF16)
    rest = x - hi.astype(F32)
    mid = rest.astype(BF16)
    low = (rest - mid.astype(F32)).astype(BF16)
    return hi, mid, low


def stack3(x):
    return jnp.concatenate(split3(x), axis=0)


def fold3(x):
    n = x.shape[0] // 3
    return x[:n] + (x[n : 2 * n] + x[2 * n :])


def columns(body):
    def step(i, carry):
        body(pl.ds(pl.multiple_of(i * 256, 256), 256))
        return carry

    lax.fori_loop(0, 6, step, 0)
    body(pl.ds(1536, 128))


def inverse_factor(packed):
    lane = lax.broadcasted_iota(jnp.int32, (8, 128), 1)
    sub = lax.broadcasted_iota(jnp.int32, (8, 128), 0)
    rows = []
    for q in range(4):
        g = pltpu.roll(packed, (32 - 32 * q) % 128, 1) if q != 1 else packed
        g = jnp.where((lane >= 32) & (lane < 64), g, 0.0)
        rows.append(g + jnp.where(lane == sub + 8 * q, 1.0, 0.0))
    for k in range(K):
        q, i = k // 8, k % 8
        row = rows[q][i : i + 1, :]
        pivot = row[:, 32 + k : 33 + k]
        inv = lax.rsqrt(pivot)
        inv = inv * (1.5 - 0.5 * pivot * inv * inv)
        row = row * inv
        for t in range(q, 4):
            col = rows[t][:, 32 + k : 33 + k] * inv
            new = rows[t] - col * row
            if t == q:
                new = jnp.where(sub > i, new, jnp.where(sub == i, row, rows[t]))
            rows[t] = new
    return jnp.concatenate(rows, axis=0)[:, 0:K]


def kernel(
    a_ref, b_ref, f_ref, r_ref, avg_ref, next_ref, rf_ref,
    ball, av, fv, rv, acc, br, psend, prs, ptot, gsum, ot,
    usend, urecv, wsend, wrs, wsum,
    lsem, ssem, rsem, u_s, u_r, one_s, one_r,
):
    z = lax.axis_index("shard")
    me = lax.axis_index("rep")

    def zat(off):
        return lax.rem(z + (off + 2 * NZ), NZ)

    def block(owner):
        return pl.ds(pl.multiple_of(owner * TB, TB), TB)

    loads = [
        pltpu.make_async_copy(b_ref.at[0], ball.at[block(z)], lsem.at[0]),
        pltpu.make_async_copy(r_ref, rv, lsem.at[1]),
        pltpu.make_async_copy(f_ref.at[0], fv, lsem.at[2]),
        pltpu.make_async_copy(a_ref.at[0], av, lsem.at[3]),
    ]
    for load in loads:
        load.start()

    barrier = pltpu.get_barrier_semaphore()

    for off in NEAR:
        pl.semaphore_signal(barrier, inc=1, device_id={"shard": zat(off)}, device_id_type=MESH)

    @pl.loop(1, NR)
    def _(d):
        pl.semaphore_signal(barrier, inc=1, device_id={"rep": lax.rem(me + d, NR)}, device_id_type=MESH)

    def wait_bytes(ref, sem):
        pltpu.make_async_copy(ref, ref, sem).wait()

    def piece(owner, part):
        return ball.at[pl.ds(pl.multiple_of(owner * TB + part * ROWS, ROWS), ROWS)]

    def ring(way, s, part):
        owner, to = (zat(-s), zat(1)) if way == 0 else (zat(s), zat(-1))
        source = piece(owner, part) if s else b_ref.at[0, pl.ds(part * ROWS, ROWS)]
        return pltpu.make_async_remote_copy(
            source, piece(owner, part), ssem.at[way, s, part], rsem.at[way, s, part],
            device_id={"shard": to}, device_id_type=MESH,
        )

    def used(way, s, part):
        return s < 7 or (s == 7 and (part < PARTS // 2) == (way == 0))

    done = [0]

    def ticks(upto):
        for k in range(done[0] - PARTS, upto - PARTS):
            s = k // PARTS
            for way in range(2):
                if s < 0:
                    ring(way, 0, k + PARTS if way == 0 else -1 - k).start()
                    continue
                part = k % PARTS if way == 0 else PARTS - 1 - k % PARTS
                if used(way, s, part):
                    ring(way, s, part).wait_recv()
                    if used(way, s + 1, part):
                        ring(way, s + 1, part).start()
        done[0] = max(done[0], upto)

    def gather_terms(offsets):
        ticks(PARTS * (max(offsets) + 1) if max(offsets) else 0)
        at = jnp.concatenate([av[block(zat(o)), :].T for o in offsets], axis=1)

        def body(cols):
            rows = jnp.concatenate([ball[block(zat(o)), cols] for o in offsets], axis=0)
            acc[:, cols] += mm(at, rows, NN)

        columns(body)

    pl.semaphore_wait(barrier, len(NEAR) + NR - 1)
    ticks(AT[0])

    loads[0].wait()
    loads[1].wait()
    r3 = stack3(rv[...])
    br[z] = fold3(mm(r3, ball[block(z), :], NT))

    def br_send(owner, off, i):
        pltpu.make_async_remote_copy(
            br.at[owner], br.at[owner], one_s.at[i], one_r.at[i],
            device_id={"shard": zat(off)}, device_id_type=MESH,
        ).start()

    for off in (3, -3):
        br_send(z, off, 8)
    for off in (1, -1):
        br_send(z, off, 9)

    loads[2].wait()
    fr = fold3(mm(r3, fv[...], NT))
    columns(lambda cols: acc.__setitem__((slice(None), cols), fv[:, cols].astype(F32)))
    ticks(AT[1])
    loads[3].wait()
    wait_bytes(br.at[pl.ds(0, 2)], one_r.at[8])
    br_send(zat(-3), 3, 10)
    br_send(zat(3), -3, 10)
    for off in (1, -1):
        for o in (3, -3):
            br_send(zat(o), off, 9)
    ticks(AT[2])
    wait_bytes(br.at[pl.ds(0, 2)], one_r.at[10])
    for off in (1, -1):
        for o in (6, -6):
            br_send(zat(o), off, 9)
    br_send(zat(-6), 2, 9)
    ticks(AT[3])
    wait_bytes(br.at[pl.ds(0, 11)], one_r.at[9])
    br3 = stack3(jnp.concatenate([br[i] for i in range(NZ)], axis=1))
    psend[...] = fr + fold3(mm(br3, av[...], NN))

    def z_first(ref, i):
        for off in (8, 4, 12):
            pltpu.make_async_remote_copy(
                ref.at[z // 4], ref.at[z // 4], one_s.at[i], one_r.at[i],
                device_id={"shard": zat(off)}, device_id_type=MESH,
            ).start()

    def z_second(ref, i):
        wait_bytes(ref.at[pl.ds(0, 3)], one_r.at[i])
        mine = 4 + lax.rem(z, 4)
        ref[mine] = (ref[0] + ref[1]) + (ref[2] + ref[3])
        for off in (2, 1, -1):
            pltpu.make_async_remote_copy(
                ref.at[mine], ref.at[mine], one_s.at[i + 1], one_r.at[i + 1],
                device_id={"shard": zat(off)}, device_id_type=MESH,
            ).start()

    def z_total(ref, i):
        wait_bytes(ref.at[pl.ds(0, 3)], one_r.at[i + 1])
        return (ref[4] + ref[5]) + (ref[6] + ref[7])

    def p_tile(o):
        return (
            pl.ds(pl.multiple_of(o // 2 * 8, 8), 8),
            pl.ds(pl.multiple_of(o % 2 * 128, 128), 128),
        )

    @pl.loop(0, P_OWNERS)
    def _(o):
        to = 4 * o

        @pl.when(to != me)
        def _():
            pltpu.make_async_remote_copy(
                psend.at[p_tile(o)], prs.at[lax.rem(me - to + (NR - 1), NR)], one_s.at[0], one_r.at[0],
                device_id={"rep": to}, device_id_type=MESH,
            ).start()

    ticks(AT[4])
    gather_terms([0])
    own_p = lax.rem(me, 4) == 0

    @pl.when(own_p)
    def _():
        wait_bytes(prs.at[pl.ds(0, NR - 1)], one_r.at[0])
        tile = p_tile(me // 4)
        ptot[tile] = jnp.sum(prs[0 : NR - 1], axis=0) + psend[tile]

        @pl.loop(1, NR)
        def _(d):
            pltpu.make_async_remote_copy(
                ptot.at[tile], ptot.at[tile], one_s.at[1], one_r.at[1],
                device_id={"rep": lax.rem(me + d, NR)}, device_id_type=MESH,
            ).start()

    ticks(AT[5])
    gather_terms([-1, 1])

    @pl.when(own_p)
    def _():
        wait_bytes(prs.at[pl.ds(0, P_OWNERS - 1)], one_r.at[1])

    @pl.when(jnp.logical_not(own_p))
    def _():
        wait_bytes(prs.at[pl.ds(0, P_OWNERS)], one_r.at[1])

    pt = ptot[...]
    p_hi, p_mid, p_low = split3(pt)
    wide = jnp.concatenate([pt] * 4, axis=0)
    w_hi, w_mid, w_low = split3(wide)
    g = mm(p_hi, w_hi, NT) + (
        (mm(p_hi, w_mid, NT) + mm(p_mid, w_hi, NT))
        + (mm(p_mid, w_mid, NT) + mm(p_hi, w_low, NT) + mm(p_low, w_hi, NT))
    )
    lane = lax.broadcasted_iota(jnp.int32, (8, 128), 1)
    packed = jnp.zeros((8, 128), F32)
    for q in range(4):
        packed = jnp.where((lane >= 32 * q) & (lane < 32 * q + 32), g[8 * q : 8 * q + 8], packed)
    gsum[z // 4] = packed
    z_first(gsum, 2)
    ticks(AT[6])
    gather_terms([-2, 2])
    z_second(gsum, 2)
    ticks(AT[7])
    l_inv = inverse_factor(z_total(gsum, 2))
    l_hi, l_mid, l_low = split3(l_inv)
    o_t = mm(l_hi, p_hi, NN) + (
        (mm(l_hi, p_mid, NN) + mm(l_mid, p_hi, NN))
        + (mm(l_mid, p_mid, NN) + mm(l_hi, p_low, NN) + mm(l_low, p_hi, NN))
    )
    ot[...] = o_t
    o3 = stack3(o_t)

    hops = [(o, o - HELD) for o in range(HELD + 1, 9)] + [(-o, HELD - o) for o in range(HELD + 1, 8)]
    hops.sort(key=lambda hop: -abs(hop[1]))

    def u_copy(i):
        return pltpu.make_async_remote_copy(
            usend.at[i], urecv.at[i], u_s.at[i], u_r.at[i],
            device_id={"shard": zat(hops[i][1])}, device_id_type=MESH,
        )

    for i, (o, _) in enumerate(hops):
        usend[i] = fold3(mm(o3, av[block(zat(o)), :], NT))
        u_copy(i).start()
    for s in range(3, HELD + 1):
        gather_terms([-s, s])
    def held_terms(cols):
        m_hi, m_mid, _ = split3(acc[:, cols])
        cross = mm(o3[: 2 * K], m_mid, NN)
        wsend[:, cols] = fold3(mm(o3, m_hi, NN)) + (cross[:K] + cross[K:])

    columns(held_terms)
    for i in range(len(hops)):
        u_copy(i).wait_recv()
    u_up = sum(urecv[i] for i in range(len(hops)) if hops[i][0] > 0)
    u_down = sum(urecv[i] for i in range(len(hops)) if hops[i][0] < 0)
    u3 = stack3(jnp.concatenate([u_up, u_down], axis=1))

    def w_chunk(q):
        return (
            pl.ds(pl.multiple_of(lax.rem(q, 2) * 16, 16), 16),
            pl.ds(pl.multiple_of(q // 2 * 128, 128), 128),
        )

    def w_terms(i, width):
        cols = pl.ds(pl.multiple_of(i * 256, 256), width)
        rows = jnp.concatenate([ball[block(zat(HELD)), cols], ball[block(zat(-HELD)), cols]], axis=0)
        wsend[:, cols] += fold3(mm(u3, rows, NN))
        for j in range(width // 64):
            q = 4 * i + j

            @pl.when(q != me)
            def _():
                pltpu.make_async_remote_copy(
                    wsend.at[w_chunk(q)], wrs.at[lax.rem(me - q + (NR - 1), NR)], one_s.at[4], one_r.at[4],
                    device_id={"rep": q}, device_id_type=MESH,
                ).start()

    @pl.loop(0, 6)
    def _(i):
        w_terms(i, 256)

    w_terms(6, 128)
    ticks(AT[8])
    own_w = me < W_OWNERS

    @pl.when(own_w)
    def _():
        wait_bytes(wrs.at[pl.ds(0, NR - 1)], one_r.at[4])
        wsum[z // 4] = jnp.sum(wrs[0 : NR - 1], axis=0) + wsend[w_chunk(me)]
        z_first(wsum, 5)

    ticks(AT[9])
    gather_terms([-5, 5])

    @pl.when(own_w)
    def _():
        z_second(wsum, 5)

    ticks(AT[10])

    @pl.when(own_w)
    def _():
        rf_ref[w_chunk(me)] = z_total(wsum, 5) * (1.0 / NR)

        @pl.loop(1, NR)
        def _(d):
            pltpu.make_async_remote_copy(
                rf_ref.at[w_chunk(me)], rf_ref.at[w_chunk(me)], one_s.at[7], one_r.at[7],
                device_id={"rep": lax.rem(me + d, NR)}, device_id_type=MESH,
            ).start()

    ticks(AT[11])
    gather_terms([-6, 6])
    ticks(AT[12])

    @pl.when(own_w)
    def _():
        wait_bytes(wrs.at[pl.ds(0, W_OWNERS - 1)], one_r.at[7])

    @pl.when(jnp.logical_not(own_w))
    def _():
        wait_bytes(wrs.at[pl.ds(0, W_OWNERS)], one_r.at[7])

    o_hi, o_mid, o_low = split3(ot[...])
    lhs = jnp.concatenate([o_hi, o_hi, o_mid, o_mid, o_hi, o_low], axis=0)

    def rebuild(cols):
        h, m, low = split3(rf_ref[:, cols])
        rebuilt = mm(lhs, jnp.concatenate([h, m, h, m, low, h], axis=0), TN)
        avg_ref[:, cols] = rebuilt.astype(BF16)
        acc[:, cols] -= rebuilt

    columns(rebuild)
    gather_terms([-7, 7])
    ticks(PARTS * 9)
    last = av[block(zat(8)), :].T

    def finish(cols):
        next_ref[0, :, cols] = (acc[:, cols] + mm(last, ball[block(zat(8)), cols], NN)).astype(BF16)

    columns(finish)

    for k in range(8 * PARTS):
        for way in range(2):
            if used(way, k // PARTS, k % PARTS):
                ring(way, k // PARTS, k % PARTS).wait_send()
    wait_bytes(br.at[pl.ds(0, 2)], one_s.at[8])
    wait_bytes(br.at[pl.ds(0, 2)], one_s.at[10])
    wait_bytes(br.at[pl.ds(0, 11)], one_s.at[9])
    for i in range(len(hops)):
        u_copy(i).wait_send()
    for i in (2, 3):
        wait_bytes(gsum.at[pl.ds(0, 3)], one_s.at[i])

    @pl.when(own_p)
    def _():
        wait_bytes(prs.at[pl.ds(0, P_OWNERS - 1)], one_s.at[0])
        wait_bytes(prs.at[pl.ds(0, NR - 1)], one_s.at[1])

    @pl.when(jnp.logical_not(own_p))
    def _():
        wait_bytes(prs.at[pl.ds(0, P_OWNERS)], one_s.at[0])

    @pl.when(own_w)
    def _():
        wait_bytes(wrs.at[pl.ds(0, W_OWNERS - 1)], one_s.at[4])
        for i in (5, 6):
            wait_bytes(wsum.at[pl.ds(0, 3)], one_s.at[i])
        wait_bytes(wrs.at[pl.ds(0, NR - 1)], one_s.at[7])

    @pl.when(jnp.logical_not(own_w))
    def _():
        wait_bytes(wrs.at[pl.ds(0, W_OWNERS)], one_s.at[4])


def store(avg_ref, next_ref, rf_ref, avg_out, next_out, rf_out, sem):
    copies = [
        pltpu.make_async_copy(avg_ref, avg_out, sem.at[0]),
        pltpu.make_async_copy(next_ref, next_out, sem.at[1]),
        pltpu.make_async_copy(rf_ref, rf_out, sem.at[2]),
    ]
    for copy in copies:
        copy.start()
    for copy in copies:
        copy.wait()


def on_device(activations, output_grad, feedback, right_start):
    n_hops = (8 - HELD) + (7 - HELD)
    dma = pltpu.SemaphoreType.DMA
    shapes = (
        jax.ShapeDtypeStruct((H, D), BF16),
        jax.ShapeDtypeStruct((1, H, D), BF16),
        jax.ShapeDtypeStruct((K, D), F32),
    )
    results = pl.pallas_call(
        kernel,
        out_shape=tuple(pltpu.VMEM(s.shape, s.dtype) for s in shapes),
        in_specs=[pl.BlockSpec(memory_space=pltpu.HBM)] * 4,
        out_specs=[pl.BlockSpec(memory_space=pltpu.VMEM)] * 3,
        scratch_shapes=[
            pltpu.VMEM((NZ * TB, D), BF16),
            pltpu.VMEM((NZ * TB, H), BF16),
            pltpu.VMEM((H, D), BF16),
            pltpu.VMEM((K, D), F32),
            pltpu.VMEM((H, D), F32),
            pltpu.VMEM((NZ, K, TB), F32),
            pltpu.VMEM((K, H), F32),
            pltpu.VMEM((NR, 8, 128), F32),
            pltpu.VMEM((K, H), F32),
            pltpu.VMEM((8, 8, 128), F32),
            pltpu.VMEM((K, H), F32),
            pltpu.VMEM((n_hops, K, TB), F32),
            pltpu.VMEM((n_hops, K, TB), F32),
            pltpu.VMEM((K, D), F32),
            pltpu.VMEM((NR, 16, 128), F32),
            pltpu.VMEM((8, 16, 128), F32),
            dma((4,)),
            dma((2, 8, PARTS)),
            dma((2, 8, PARTS)),
            dma((n_hops,)),
            dma((n_hops,)),
            dma((11,)),
            dma((11,)),
        ],
        compiler_params=pltpu.CompilerParams(
            collective_id=0, has_side_effects=True, vmem_limit_bytes=61 * 2**20
        ),
        cost_estimate=pl.CostEstimate(
            flops=2 * H * NZ * TB * D, bytes_accessed=5_000_000, transcendentals=0
        ),
    )(activations, output_grad, feedback, right_start.T)
    averaged, feedback_next, right_t = pl.pallas_call(
        store,
        out_shape=shapes,
        in_specs=[pl.BlockSpec(memory_space=pl.ANY)] * 3,
        out_specs=[pl.BlockSpec(memory_space=pltpu.HBM)] * 3,
        scratch_shapes=[dma((3,))],
        compiler_params=pltpu.CompilerParams(vmem_limit_bytes=2**20),
    )(*results)
    return averaged, feedback_next, right_t.T


def solution(mesh):
    return jax.shard_map(
        on_device,
        mesh=mesh,
        in_specs=(P("rep", None, "shard"), P("rep", "shard", None), P("rep", "shard", None), P()),
        out_specs=(P("shard", None), P("rep", "shard", None), P()),
        check_vma=False,
    )
```
